256 devices in a mesh: ctx: 32 (over y_hi, z, core), head: 8 (over x, y_lo).
Axes of the slice: x: 4, y: 4 (y_hi: 2, y_lo: 2; y = y_hi * 2 + y_lo), z: 8, core: 2. Of those that a mesh axis runs over, the one named last changes fastest.
Arguments:
- query_heads: bfloat16 [2, 16384, 4096], P(None, 'ctx', 'head'), may hold values from -140 to 140
- key_heads: bfloat16 [2, 16384, 1024], P(None, 'ctx', 'head'), may hold values from -6 to 6
- value_heads: bfloat16 [2, 16384, 1024], P(None, 'ctx', 'head'), may hold values from -6 to 6
- doc_start: int32 [2, 16384], P(None, 'ctx'), may hold values from 0 to 32767, as said below
- out_weight: bfloat16 [4096, 4096], P('head'), may hold values from -0.125 to 0.125
Outputs:
- layer_output: bfloat16 [2, 16384, 4096], P(None, 'ctx', 'head')
The draws below stay inside these ranges and needn't reach their ends.
Inputs may be any that keep to these rules, and one draw needn't show every extreme that they name: `doc_start`: documents are contiguous runs of positions; positions 0 and 32767 each begin one; each token holds the first position of its own document, which is at most its own position.
All inputs are finite; a program needn't handle non-finite values.
Results may differ from the reference program's by a relative error of at most 0.017.
Values may be sent and summed in bfloat16 or wider, within the bound.
No kernel may reach another device: no remote copies, remote signals or barrier semaphores. Data moves between devices by JAX's collectives and lax.ppermute only.
A program may use at most 128 MiB of HBM per device.

```python
import jax
import jax.numpy as jnp
from jax import lax

QH = 32
KVH = 8
HD = 128
D = 4096
BLK = 512
WSTEPS = 4
SEQH = 16384
SEQ = 32768
WIN = 2048
N_CTX = 32
N_HEAD = 8


def shared_keys(key):
    return jnp.clip(jax.random.normal(key, (2, SEQH, KVH * HD), jnp.float32), -6.0, 6.0)


def draw_key_heads(key, part):
    base_keys = shared_keys(key)
    return base_keys.astype(jnp.bfloat16)


def draw_query_heads(key, part):
    key = jax.random.fold_in(key, 7)
    drawn = jnp.clip(jax.random.normal(key, (2, SEQH, QH * HD), jnp.float32), -6.0, 6.0)
    return drawn.astype(jnp.bfloat16)


def draw_doc_start(key, part):
    key = jax.random.fold_in(key, 5)
    position = jnp.arange(SEQ, dtype=jnp.int32)
    starts_here = jax.random.randint(key, (SEQ,), 0, 4 * BLK) == 0
    starts_here = starts_here | (position == 0) | (position == SEQ - 1)
    doc_first = lax.cummax(jnp.where(starts_here, position, 0), axis=0)
    first = doc_first[:SEQH]
    second = doc_first[SEQH:].reshape(SEQH // BLK, BLK)[::-1].reshape(SEQH)
    return jnp.stack([first, second], axis=0).astype(jnp.int32)


def strengthened(values, stream_key, source, target, parts, factor):
    def block_of(dim):
        return (jnp.arange(values.shape[dim]) // (values.shape[dim] // parts)).reshape((-1,) + (1,) * (values.ndim - 1 - dim))

    one_side = jax.random.permutation(stream_key, parts)[block_of(target)]
    second = (block_of(target) + parts // 2) % parts
    return jnp.where((block_of(source) == one_side) | (block_of(source) == second), factor * values, values)


def levels(own_key, shape, pieces, low, top_value):
    def one(dim, shards_of):
        heights = jax.random.uniform(jax.random.fold_in(jax.random.fold_in(own_key, 6), dim), (shards_of,), jnp.float32, low / len(pieces), top_value / len(pieces))
        return jnp.repeat(jnp.exp(heights), shape[dim] // shards_of).reshape((-1,) + (1,) * (len(shape) - dim - 1))

    loudness = one(*pieces[0])
    for cut in pieces[1:]:
        loudness = loudness * one(*cut)
    return loudness


def centred(stream_key, dims, width, limit, shards=(), kind=jnp.bfloat16):
    values = jax.random.normal(stream_key, dims, jnp.float32) * width
    if len(shards) > 0:
        values = levels(stream_key, dims, shards, -0.22, 0.18) * values
    return jnp.clip(values, min=-limit, max=limit).astype(kind)


def bell_draw_with(own_key, shape, deviation, most, cuts, heavy, held_as=jnp.bfloat16):
    result = deviation * jax.random.normal(own_key, shape, jnp.float32)
    if cuts:
        result = result * levels(own_key, shape, cuts, -0.22, 0.18)
    return jnp.clip(strengthened(result, jax.random.fold_in(own_key, 3), *heavy), -most, most).astype(held_as)


def setup_inputs(seed: int = 0) -> dict:
    splits = jax.random.split(jax.random.key(seed), 6)
    return {
        "query_heads": draw_query_heads(jax.random.fold_in(splits[5], 71), 0),
        "key_heads": draw_key_heads(jax.random.fold_in(splits[5], 71), 0),
        "value_heads": centred(splits[2], (2, SEQH, KVH * HD), 1.0, 6.0, ((1, 32), (2, 8))),
        "doc_start": draw_doc_start(jax.random.fold_in(splits[5], 71), 0),
        "out_weight": bell_draw_with(splits[4], (QH * HD, D), (QH * HD) ** -0.5, 0.125, ((0, 8),), (0, 1, 8, 2.0)),
    }


def natural_order(array):
    first = array[0]
    second = array[1].reshape((N_CTX, BLK) + array.shape[2:])[::-1].reshape((SEQH,) + array.shape[2:])
    return jnp.concatenate([first, second], axis=0)


def split_order(array):
    first = array[:SEQH]
    second = array[SEQH:].reshape((N_CTX, BLK) + array.shape[1:])[::-1].reshape((SEQH,) + array.shape[1:])
    return jnp.stack([first, second], axis=0)


def reference(query_heads, key_heads, value_heads, doc_start, out_weight):
    per_group = QH // KVH
    query_seq = natural_order(query_heads)
    key_seq = natural_order(key_heads)
    value_seq = natural_order(value_heads)
    first_seq = natural_order(doc_start)
    lead = WSTEPS * BLK
    padded_keys = jnp.concatenate([jnp.zeros((lead, KVH * HD), key_heads.dtype), key_seq], axis=0)
    padded_values = jnp.concatenate([jnp.zeros((lead, KVH * HD), value_heads.dtype), value_seq], axis=0)
    row_offsets = jnp.arange(BLK, dtype=jnp.int32)
    key_offsets = jnp.arange((WSTEPS + 1) * BLK, dtype=jnp.int32)
    scale = HD ** -0.5

    def one_block(block_index):
        begin = block_index * BLK
        queries = lax.dynamic_slice_in_dim(query_seq, begin, BLK, 0).astype(jnp.float32).reshape(BLK, KVH, per_group, HD)
        keys_here = lax.dynamic_slice_in_dim(padded_keys, begin, (WSTEPS + 1) * BLK, 0).astype(jnp.float32).reshape(-1, KVH, HD)
        values_here = lax.dynamic_slice_in_dim(padded_values, begin, (WSTEPS + 1) * BLK, 0).astype(jnp.float32).reshape(-1, KVH, HD)
        first_pos = lax.dynamic_slice_in_dim(first_seq, begin, BLK, 0)
        query_pos = begin + row_offsets
        key_pos = begin - lead + key_offsets
        allowed = (key_pos[None, :] >= first_pos[:, None]) & (key_pos[None, :] <= query_pos[:, None]) & (query_pos[:, None] - key_pos[None, :] < WIN)
        scores = jnp.einsum("tgrd,lgd->grtl", queries, keys_here, precision=lax.Precision.HIGHEST) * scale
        highest = jnp.max(jnp.where(allowed, scores, -1e30), axis=-1, keepdims=True)
        weights = jnp.where(allowed, jnp.exp(scores - highest), 0.0)
        weight_sum = jnp.sum(weights, axis=-1)
        rounded = lax.optimization_barrier(weights.astype(jnp.bfloat16)).astype(jnp.float32)
        mixed = jnp.einsum("grtl,lgd->tgrd", rounded, values_here, precision=lax.Precision.HIGHEST)
        mixed = mixed / jnp.transpose(weight_sum, (2, 0, 1))[..., None]
        return mixed.reshape(BLK, QH * HD).astype(jnp.bfloat16)

    attended = lax.map(one_block, jnp.arange(SEQ // BLK, dtype=jnp.int32)).reshape(SEQ, QH * HD)
    columns = QH * HD // N_HEAD
    summed = jnp.zeros((SEQ, D), jnp.float32)
    for member in range(N_HEAD):
        product = jnp.dot(attended[:, member * columns:(member + 1) * columns], out_weight[member * columns:(member + 1) * columns], preferred_element_type=jnp.float32)
        rounded_part = lax.optimization_barrier(product.astype(jnp.bfloat16))
        summed = summed + rounded_part.astype(jnp.float32)
    return split_order(summed.astype(jnp.bfloat16))
```

```python
import functools
import math

import jax
import jax.numpy as jnp
from jax import lax
from jax.experimental import pallas as pl
from jax.experimental.pallas import tpu as pltpu
from jax.sharding import PartitionSpec as P

HD = 128
LAGS = 4
TILE = 256
NEG = -1e30
NT = (((1,), (1,)), ((), ()))
NN = (((1,), (0,)), ((), ()))
VMEM = pl.BlockSpec(memory_space=pltpu.VMEM)
SMEM = pl.BlockSpec(memory_space=pltpu.SMEM)
F32 = jnp.float32
BF16 = jnp.bfloat16


def mm(a, b, dims=NN):
    return lax.dot_general(a, b, dims, preferred_element_type=F32)


def attn_kernel(
    info_ref, q_ref, doc_ref, own_ref, swap0_ref, near_ref, swap1_ref, far_ref, swap2_ref,
    o_ref, kk, vv, sbuf,
):
    blk = own_ref.shape[1]
    heads = q_ref.shape[1] // HD
    base = info_ref[0]
    hard = info_ref[1] == 1

    def fill(lag, ref):
        rows = pl.ds(lag * blk, blk)
        k = ref[0]
        kk[rows, :HD] = k
        kk[rows, HD:] = k
        vv[rows, :HD] = ref[1]
        vv[rows, HD:] = jnp.ones((blk, HD), BF16)

    fill(0, own_ref)
    fill(2, near_ref)
    fill(4, far_ref)

    @pl.when(hard)
    def _():
        fill(1, swap1_ref)
        fill(3, swap2_ref)

    @pl.when(jnp.logical_not(hard))
    def _():
        fill(1, swap0_ref)
        fill(3, swap1_ref)

    factor = HD ** -0.5 * math.log2(math.e)
    tiles = blk // TILE
    for t in range(tiles):
        r0 = t * TILE
        rel = doc_ref[r0:r0 + TILE, :] - base
        col = lax.broadcasted_iota(jnp.int32, (TILE, blk), 1)
        row_t = lax.broadcasted_iota(jnp.int32, (TILE, TILE), 0)
        col_t = lax.broadcasted_iota(jnp.int32, (TILE, TILE), 1)
        tri = col_t <= row_t
        for a in range(heads):
            sb = sbuf.at[(t * heads + a) % 2]
            qf = q_ref[r0:r0 + TILE, a * HD:(a + 1) * HD].astype(F32) * factor
            hi = qf.astype(BF16)
            lo = (qf - hi.astype(F32)).astype(BF16)
            qq = jnp.concatenate([hi, lo], axis=1)

            def scores(first, count):
                return mm(qq, kk[first:first + count, :], NT)

            def running(m, s):
                for x in range(s.shape[1] // HD):
                    p = s[:, x * HD:(x + 1) * HD]
                    m = p if m is None else jnp.maximum(m, p)
                return m

            m = None
            pieces = []
            off = 0
            for lag in (3, 2, 1):
                s = jnp.where(col - lag * blk >= rel, scores(lag * blk, blk), NEG)
                m = running(m, s)
                sb[:, off:off + blk] = s
                pieces.append((off, blk, lag * blk))
                off += blk
            for u in range(tiles):
                if u == t:
                    continue
                lag = 0 if u < t else LAGS
                first = lag * blk + u * TILE
                s = jnp.where(col_t + (u * TILE - lag * blk) >= rel, scores(first, TILE), NEG)
                m = running(m, s)
                sb[:, off:off + TILE] = s
                pieces.append((off, TILE, first))
                off += TILE
            far = LAGS * blk
            s = jnp.where(tri, scores(r0, TILE), scores(far + r0, TILE))
            position = jnp.where(tri, col_t + r0, col_t + (r0 - far))
            s = jnp.where(position >= rel, s, NEG)
            m = running(m, s)
            sb[:, off:off + TILE] = s
            top = jnp.max(m, axis=1, keepdims=True)
            acc = jnp.zeros((TILE, 2 * HD), F32)
            for begin, count, first in pieces:
                p = jnp.exp2(sb[:, begin:begin + count] - top).astype(BF16)
                acc = acc + mm(p, vv[first:first + count, :])
            p = jnp.exp2(sb[:, off:off + TILE] - top).astype(BF16)
            zero = jnp.zeros_like(p)
            acc = acc + mm(jnp.where(tri, p, zero), vv[r0:r0 + TILE, :])
            acc = acc + mm(jnp.where(tri, zero, p), vv[far + r0:far + r0 + TILE, :])
            o_ref[r0:r0 + TILE, a * HD:(a + 1) * HD] = (acc[:, :HD] / acc[:, HD:]).astype(BF16)


def attention(name, info, q, doc, *blocks):
    rows, cols = q.shape
    keys = (LAGS + 1) * rows
    flops = 4 * rows * cols * keys
    return pl.pallas_call(
        attn_kernel,
        out_shape=jax.ShapeDtypeStruct((rows, cols), BF16),
        in_specs=[SMEM] + [VMEM] * (2 + len(blocks)),
        out_specs=VMEM,
        scratch_shapes=[
            pltpu.VMEM((keys, 2 * HD), BF16),
            pltpu.VMEM((keys, 2 * HD), BF16),
            pltpu.VMEM((2, TILE, LAGS * rows), F32),
        ],
        compiler_params=pltpu.CompilerParams(vmem_limit_bytes=40 * 2**20),
        cost_estimate=pl.CostEstimate(
            flops=4 * flops, bytes_accessed=4 * 2**20, transcendentals=rows * cols // HD * keys
        ),
        name=name,
    )(info, q, doc, *blocks)


def halves(core, rows):
    h = rows // 2
    return pl.ds(pl.multiple_of(core * h, h), h), pl.ds(pl.multiple_of((1 - core) * h, h), h)


def gather_first_kernel(
    info_ref, own_ref, left_ref, right_ref, fa_ref, fb_ref, w_ref,
    wl_ref, wlp_ref, wr_ref, wrp_ref, wf_ref, wfp_ref, send_ref, keep_ref,
):
    x, y, core = info_ref[0], info_ref[1], info_ref[2]
    rows, width = own_ref.shape
    mine, other = halves(core, width)
    cut = rows // 2

    def block(side, r):
        wide = pl.ds(pl.multiple_of(side * width, width), width)
        own_cols = pl.ds(pl.multiple_of((2 * x + side) * width, width), width)
        acc = mm(own_ref[r, :], w_ref[:, own_cols])
        for ref, wm, wp in ((left_ref, wl_ref, wlp_ref), (right_ref, wr_ref, wrp_ref)):
            acc = acc + mm(ref[r, mine], wm[:, wide])
            acc = acc + mm(ref[r, other], wp[:, wide])
        ref = fa_ref if r.start == 0 else fb_ref
        acc = acc + mm(ref[:, mine], wf_ref[:, wide])
        acc = acc + mm(ref[:, other], wfp_ref[:, wide])
        return acc.astype(BF16)

    for r in (slice(0, cut), slice(cut, rows)):
        send_ref[r, :] = block(1 - y, r)
    for r in (slice(0, cut), slice(cut, rows)):
        keep_ref[r, :] = block(y, r)


def reduce_first_kernel(
    info_ref, own_ref, peer_ref, w_ref, wm_ref, wp_ref, fa_ref, fb_ref, up_ref, down_ref, keep_ref
):
    x, y, core = info_ref[0], info_ref[1], info_ref[2]
    rows, width = own_ref.shape
    mine, other = halves(core, width)
    cut = rows // 2
    h = width // 2

    def block(target, r):
        own_cols = pl.ds(pl.multiple_of((2 * target + y) * width, width), width)
        w_rows = pl.ds(pl.multiple_of(target * h, h), h)
        acc = mm(own_ref[r, :], w_ref[:, own_cols])
        acc = acc + mm(peer_ref[r, mine], wm_ref[w_rows, :])
        acc = acc + mm(peer_ref[r, other], wp_ref[w_rows, :])
        return acc.astype(BF16)

    lower, upper = slice(0, cut), slice(cut, rows)
    ring = 4
    opposite = lax.rem(x + 2, ring)
    fa_ref[...] = block(opposite, lower)
    fb_ref[...] = block(opposite, upper)
    for ref, target in (
        (up_ref, lax.rem(x + 1, ring)), (down_ref, lax.rem(x + ring - 1, ring)), (keep_ref, x)
    ):
        for r in (lower, upper):
            ref[r, :] = block(target, r)


def project(kernel, name, outs, args, flops):
    return pl.pallas_call(
        kernel,
        out_shape=[jax.ShapeDtypeStruct(s, BF16) for s in outs],
        in_specs=[SMEM] + [VMEM] * (len(args) - 1),
        out_specs=[VMEM] * len(outs),
        compiler_params=pltpu.CompilerParams(vmem_limit_bytes=40 * 2**20),
        cost_estimate=pl.CostEstimate(flops=2 * flops, bytes_accessed=10 * 2**20, transcendentals=0),
        name=name,
    )(*args)


def on_device(query_heads, key_heads, value_heads, doc_start, out_weight):
    ctx_size = lax.axis_size("ctx")
    c = lax.axis_index("ctx")
    head = lax.axis_index("head")
    core = c % 2
    x, y = head // 2, head % 2
    ring = lax.axis_size("head") // 2
    blk = key_heads.shape[1]
    width = query_heads.shape[2]

    def ctx_move(array, to):
        return lax.ppermute(
            array, "ctx", [(i, to(i)) for i in range(ctx_size) if 0 <= to(i) < ctx_size]
        )

    def head_move(array, to):
        return lax.ppermute(array, "head", [(i, to(i)) for i in range(2 * ring)])

    def swap(array):
        return ctx_move(array, lambda i: i ^ 1)

    def plus(array):
        return head_move(array, lambda i: (i + 2) % (2 * ring))

    def minus(array):
        return head_move(array, lambda i: (i - 2) % (2 * ring))

    def across(array):
        return head_move(array, lambda i: (i + 4) % (2 * ring))

    def mirror(array):
        return head_move(array, lambda i: i ^ 1)

    kv = jnp.stack([key_heads, value_heads], axis=1)
    near0 = ctx_move(kv[0], lambda i: i + 2)
    near1 = ctx_move(kv[1], lambda i: i - 2)
    traded = swap(kv)
    last = c >= ctx_size - 2

    def piece(col_start, cols):
        return lax.dynamic_slice(
            out_weight, (core * (width // 2), col_start), (width // 2, cols)
        )

    w_left = plus(piece(((x + 1) % ring) * 2 * width, 2 * width))
    w_right = minus(piece(((x - 1) % ring) * 2 * width, 2 * width))
    w_far = across(piece(((x + 2) % ring) * 2 * width, 2 * width))
    w_peer = mirror(
        jnp.concatenate([piece((2 * i + 1 - y) * width, width) for i in range(ring)], axis=0)
    )

    near1 = jnp.where(last, traded[0], near1)
    far0 = ctx_move(near0, lambda i: i + 2)
    far1 = ctx_move(near1, lambda i: i - 2)
    near0_traded = swap(near0)
    near1_traded = swap(near1)
    far1 = jnp.where(last, near0_traded, far1)
    far_traded = swap(jnp.where(core == 0, far1, far0))

    def attend(half, near, far, near_traded):
        block = c if half == 0 else 2 * ctx_size - 1 - c
        info = jnp.stack([block * blk, (core == half).astype(jnp.int32)]).astype(jnp.int32)
        return attention(
            "attend" + str(half), info, query_heads[half], doc_start[half][:, None],
            kv[half], traded[half], near, near_traded, far, far_traded,
        )

    info = jnp.stack([x, y, core]).astype(jnp.int32)
    cut = blk // 2
    mixed0 = attend(0, near0, far0, near0_traded)
    left = plus(mixed0)
    right = minus(mixed0)
    mixed1 = attend(1, near1, far1, near1_traded)
    peer = mirror(mixed1)
    opposite_a = plus(left[:cut])
    opposite_b = minus(right[cut:])

    w_left2, w_right2, w_far2, w_peer2 = swap(w_left), swap(w_right), swap(w_far), swap(w_peer)

    fa, fb, up, down, keep1 = project(
        reduce_first_kernel, "reduce_first",
        [(cut, width), (cut, width)] + [(blk, width)] * 3,
        [info, mixed1, peer, out_weight, w_peer, w_peer2],
        2 * blk * width * 8 * width,
    )
    got_a = plus(fa)
    got_b = minus(fb)
    send, keep0 = project(
        gather_first_kernel, "gather_first",
        [(blk, width)] * 2,
        [info, mixed0, left, right, opposite_a, opposite_b, out_weight,
         w_left, w_left2, w_right, w_right2, w_far, w_far2],
        2 * blk * width * 8 * width,
    )
    got0 = mirror(send)
    up = jnp.concatenate([(up[:cut].astype(F32) + got_a.astype(F32)).astype(BF16), up[cut:]], axis=0)
    down = jnp.concatenate([down[:cut], (down[cut:].astype(F32) + got_b.astype(F32)).astype(BF16)], axis=0)
    got_up = plus(up)
    got_down = minus(down)
    out0 = (keep0.astype(F32) + got0.astype(F32)).astype(BF16)
    out1 = (keep1.astype(F32) + got_up.astype(F32) + got_down.astype(F32)).astype(BF16)
    return jnp.stack([out0, out1], axis=0)


def solution(mesh):
    in_specs = (
        P(None, "ctx", "head"),
        P(None, "ctx", "head"),
        P(None, "ctx", "head"),
        P(None, "ctx"),
        P("head", None),
    )
    out_specs = P(None, "ctx", "head")
    return jax.shard_map(
        on_device, mesh=mesh, in_specs=in_specs, out_specs=out_specs, check_vma=False
    )
```

```python
import functools
import math

import jax
import jax.numpy as jnp
from jax import lax
from jax.experimental import pallas as pl
from jax.experimental.pallas import tpu as pltpu
from jax.sharding import PartitionSpec as P

HD = 128
LAGS = 4
TILE = 256
NEG = -1e30
NT = (((1,), (1,)), ((), ()))
NN = (((1,), (0,)), ((), ()))
VMEM = pl.BlockSpec(memory_space=pltpu.VMEM)
SMEM = pl.BlockSpec(memory_space=pltpu.SMEM)
STEP = 10**9
SMALL = pl.CostEstimate(flops=1, bytes_accessed=1, transcendentals=0)
F32 = jnp.float32
BF16 = jnp.bfloat16


def mm(a, b, dims=NN):
    return lax.dot_general(a, b, dims, preferred_element_type=F32)


def attn_kernel(
    half, info_ref, q_ref, doc_ref, own_ref, traded_ref, near_ref, near_traded_ref, far_ref,
    far_traded_ref, fold_near_ref, fold_traded_ref, *refs,
):
    *out_refs, kk, vv, sbuf = refs
    blk = own_ref.shape[1]
    heads = q_ref.shape[2] // HD
    base = info_ref[0]
    hard = info_ref[1] == 1
    easy = info_ref[1] == 0

    def fill(lag, ref):
        rows = pl.ds(lag * blk, blk)
        k = ref[0]
        kk[rows, :HD] = k
        kk[rows, HD:] = k
        vv[rows, :HD] = ref[1]
        vv[rows, HD:] = jnp.ones((blk, HD), BF16)

    def choose(lag, cases):
        for condition, ref in cases:
            pl.when(condition)(functools.partial(fill, lag, ref))

    fill(0, own_ref)
    fill(2, near_ref)
    choose(1, ((hard, near_traded_ref), (easy, traded_ref)))
    if half == 0:
        fill(4, far_ref)
        choose(3, ((hard, far_traded_ref), (easy, near_traded_ref)))
    else:
        folded = info_ref[2] == 1
        plain = info_ref[2] == 0
        choose(4, ((folded, fold_traded_ref), (plain, far_ref)))
        choose(3, (
            (jnp.logical_and(hard, plain), far_traded_ref),
            (jnp.logical_and(hard, folded), fold_near_ref),
            (easy, near_traded_ref),
        ))

    factor = HD ** -0.5 * math.log2(math.e)
    tiles = blk // TILE
    far = LAGS * blk
    for t in range(tiles):
        r0 = t * TILE
        rel = doc_ref[r0:r0 + TILE, :] - base
        col = lax.broadcasted_iota(jnp.int32, (TILE, blk), 1)
        row_t = lax.broadcasted_iota(jnp.int32, (TILE, TILE), 0)
        col_t = lax.broadcasted_iota(jnp.int32, (TILE, TILE), 1)
        tri = col_t <= row_t
        for a in range(heads):
            sb = sbuf.at[(t * heads + a) % 2]
            qf = q_ref[half, r0:r0 + TILE, a * HD:(a + 1) * HD].astype(F32) * factor
            hi = qf.astype(BF16)
            lo = (qf - hi.astype(F32)).astype(BF16)
            qq = jnp.concatenate([hi, lo], axis=1)

            def scores(first, count):
                return mm(qq, kk[first:first + count, :], NT)

            def running(m, s):
                for x in range(s.shape[1] // HD):
                    p = s[:, x * HD:(x + 1) * HD]
                    m = p if m is None else jnp.maximum(m, p)
                return m

            m = None
            pieces = []
            off = 0
            for lag in (3, 2, 1):
                s = jnp.where(col - lag * blk >= rel, scores(lag * blk, blk), NEG)
                m = running(m, s)
                sb[:, off:off + blk] = s
                pieces.append((off, blk, lag * blk))
                off += blk
            for u in range(tiles):
                if u == t:
                    continue
                lag = 0 if u < t else LAGS
                first = lag * blk + u * TILE
                s = jnp.where(col_t + (u * TILE - lag * blk) >= rel, scores(first, TILE), NEG)
                m = running(m, s)
                sb[:, off:off + TILE] = s
                pieces.append((off, TILE, first))
                off += TILE
            s = jnp.where(tri, scores(r0, TILE), scores(far + r0, TILE))
            position = jnp.where(tri, col_t + r0, col_t + (r0 - far))
            s = jnp.where(position >= rel, s, NEG)
            m = running(m, s)
            sb[:, off:off + TILE] = s
            top = jnp.max(m, axis=1, keepdims=True)
            acc = jnp.zeros((TILE, 2 * HD), F32)
            for begin, count, first in pieces:
                p = jnp.exp2(sb[:, begin:begin + count] - top).astype(BF16)
                acc = acc + mm(p, vv[first:first + count, :])
            p = jnp.exp2(sb[:, off:off + TILE] - top).astype(BF16)
            zero = jnp.zeros_like(p)
            acc = acc + mm(jnp.where(tri, p, zero), vv[r0:r0 + TILE, :])
            acc = acc + mm(jnp.where(tri, zero, p), vv[far + r0:far + r0 + TILE, :])
            result = (acc[:, :HD] / acc[:, HD:]).astype(BF16)
            count = out_refs[0].shape[0]
            out_refs[r0 // count][r0 % count:r0 % count + TILE, a * HD:(a + 1) * HD] = result


def attention(half, outs, info, q, doc, *blocks):
    _, rows, cols = q.shape
    keys = (LAGS + 1) * rows
    return pl.pallas_call(
        functools.partial(attn_kernel, half),
        out_shape=[jax.ShapeDtypeStruct((rows // outs, cols), BF16)] * outs,
        in_specs=[SMEM] + [VMEM] * (2 + len(blocks)),
        out_specs=[VMEM] * outs,
        scratch_shapes=[
            pltpu.VMEM((keys, 2 * HD), BF16),
            pltpu.VMEM((keys, 2 * HD), BF16),
            pltpu.VMEM((2, TILE, LAGS * rows), F32),
        ],
        compiler_params=pltpu.CompilerParams(vmem_limit_bytes=16 * 2**20),
        cost_estimate=pl.CostEstimate(flops=4 * 10**9, bytes_accessed=1, transcendentals=0) if half == 0 else pl.CostEstimate(
            flops=16 * rows * cols * keys, bytes_accessed=4 * 2**20,
            transcendentals=rows * cols // HD * keys,
        ),
        name="attend" + str(half),
    )(info, q, doc, *blocks)


def weights_kernel(info_ref, w_ref, side_ref, far_ref, peer_ref):
    x, y, core = info_ref[0], info_ref[1], info_ref[2]
    rows, wide = far_ref.shape
    width = wide // 2
    ring = peer_ref.shape[0] // rows
    mine = pl.ds(pl.multiple_of(core * rows, rows), rows)

    def columns(first, count):
        return pl.ds(pl.multiple_of(first * count, count), count)

    side_ref[...] = w_ref[:, columns(lax.rem(x + 1 + (ring - 2) * core, ring), wide)]
    far_ref[...] = w_ref[mine, columns(lax.rem(x + 2, ring), wide)]
    for i in range(ring):
        peer_ref[i * rows:(i + 1) * rows, :] = w_ref[mine, columns(2 * i + 1 - y, width)]


def split_weights(info, w, ring):
    rows, cols = w.shape
    return pl.pallas_call(
        weights_kernel,
        out_shape=[
            jax.ShapeDtypeStruct((rows, cols // ring), BF16),
            jax.ShapeDtypeStruct((rows // 2, cols // ring), BF16),
            jax.ShapeDtypeStruct((rows // 2 * ring, cols // ring // 2), BF16),
        ],
        in_specs=[SMEM, VMEM],
        out_specs=[VMEM] * 3,
        compiler_params=pltpu.CompilerParams(vmem_limit_bytes=16 * 2**20),
        cost_estimate=SMALL,
        name="split_weights",
    )(info, w)


def halves(core, rows):
    h = rows // 2
    return pl.ds(pl.multiple_of(core * h, h), h), pl.ds(pl.multiple_of((1 - core) * h, h), h)


def gather_first_kernel(
    info_ref, own_ref, left_ref, right_ref, far_ref, w_ref,
    ws_ref, wsp_ref, wf_ref, wfp_ref, send_ref, keep_ref,
):
    x, y, core = info_ref[0], info_ref[1], info_ref[2]
    rows, width = own_ref.shape
    mine, other = halves(core, width)
    cut = rows // 2

    def block(side, r):
        wide = pl.ds(pl.multiple_of(side * width, width), width)
        own_cols = pl.ds(pl.multiple_of((2 * x + side) * width, width), width)
        left, right = left_ref[r, :], right_ref[r, :]
        acc = mm(own_ref[r, :], w_ref[:, own_cols])
        acc = acc + mm(jnp.where(core == 0, left, right), ws_ref[:, wide])
        acc = acc + mm(jnp.where(core == 0, right, left), wsp_ref[:, wide])
        acc = acc + mm(far_ref[r, mine], wf_ref[:, wide])
        acc = acc + mm(far_ref[r, other], wfp_ref[:, wide])
        return acc.astype(BF16)

    for r in (slice(0, cut), slice(cut, rows)):
        send_ref[r, :] = block(1 - y, r)
    for r in (slice(0, cut), slice(cut, rows)):
        keep_ref[r, :] = block(y, r)


def targets(x, ring):
    return lax.rem(x + 2, ring), lax.rem(x + 1, ring), lax.rem(x + ring - 1, ring), x


def own_part_kernel(info_ref, own_ref, w_ref, part_ref):
    x, y = info_ref[0], info_ref[1]
    width = own_ref.shape[1]
    for i, target in enumerate(targets(x, part_ref.shape[0])):
        cols = pl.ds(pl.multiple_of((2 * target + y) * width, width), width)
        part_ref[i] = mm(own_ref[...], w_ref[:, cols])


def reduce_first_kernel(
    info_ref, peer_ref, part_ref, wm_ref, wp_ref, far_ref, up_ref, down_ref, keep_ref
):
    x, core = info_ref[0], info_ref[2]
    rows, width = peer_ref.shape
    mine, other = halves(core, width)
    h = width // 2
    ring = part_ref.shape[0]
    for i, (ref, target) in enumerate(
        zip((far_ref, up_ref, down_ref, keep_ref), targets(x, ring))
    ):
        w_rows = pl.ds(pl.multiple_of(target * h, h), h)
        for r in (slice(0, rows // 2), slice(rows // 2, rows)):
            acc = part_ref[i, r, :] + mm(peer_ref[r, mine], wm_ref[w_rows, :])
            ref[r, :] = (acc + mm(peer_ref[r, other], wp_ref[w_rows, :])).astype(BF16)


def total_kernel(info_ref, first_ref, *refs):
    *more, o_ref = refs
    total = first_ref[...].astype(F32)
    for ref in more:
        total = total + ref[...].astype(F32)
    o_ref[...] = total.astype(BF16)


def finish_kernel(info_ref, keep_ref, got_ref, done_ref, o_ref):
    o_ref[0] = (keep_ref[...].astype(F32) + got_ref[...].astype(F32)).astype(BF16)
    o_ref[1] = done_ref[...]


def project(kernel, name, outs, args, cost=0):
    return pl.pallas_call(
        kernel,
        out_shape=outs,
        in_specs=[SMEM] + [VMEM] * (len(args) - 1),
        out_specs=[VMEM] * len(outs),
        compiler_params=pltpu.CompilerParams(vmem_limit_bytes=16 * 2**20),
        cost_estimate=pl.CostEstimate(flops=cost, bytes_accessed=1, transcendentals=0),
        name=name,
    )(*args)


def after(array, *others):
    return lax.optimization_barrier((array, *others))[0]


def on_device(query_heads, key_heads, value_heads, doc_start, out_weight):
    ctx_size = lax.axis_size("ctx")
    c = lax.axis_index("ctx")
    head = lax.axis_index("head")
    core = c % 2
    x, y = head // 2, head % 2
    ring = lax.axis_size("head") // 2
    blk = key_heads.shape[1]
    width = query_heads.shape[2]

    def ctx_move(array, to):
        return lax.ppermute(
            array, "ctx", [(i, to(i)) for i in range(ctx_size) if 0 <= to(i) < ctx_size]
        )

    def head_move(array, to):
        return lax.ppermute(array, "head", [(i, to(i)) for i in range(2 * ring)])

    def swap(array):
        return ctx_move(array, lambda i: i ^ 1)

    def plus(array):
        return head_move(array, lambda i: (i + 2) % (2 * ring))

    def minus(array):
        return head_move(array, lambda i: (i - 2) % (2 * ring))

    def across(array):
        return head_move(array, lambda i: (i + 4) % (2 * ring))

    def mirror(array):
        return head_move(array, lambda i: i ^ 1)

    kv0 = jnp.stack([key_heads[0], value_heads[0]])
    kv1 = jnp.stack([key_heads[1], value_heads[1]])
    near0 = ctx_move(kv0, lambda i: i + 2)
    near1 = ctx_move(kv1, lambda i: i - 2)
    traded0 = swap(kv0)
    traded1 = swap(kv1)

    place = jnp.stack([x, y, core]).astype(jnp.int32)
    w_side, w_far, w_peer = split_weights(place, out_weight, ring)
    heads = 2 * ring
    w_side, w_far = after(w_side, traded0, traded1), after(w_far, traded0, traded1)
    w_side = lax.ppermute(w_side, ("ctx", "head"), [
        (i * heads + j, i * heads + (j + (2 if i % 2 == 0 else heads - 2)) % heads)
        for i in range(ctx_size) for j in range(heads)
    ])
    w_far = across(w_far)

    last = c >= ctx_size - 2
    near0 = after(near0, near1, traded0, traded1, w_peer)
    far0 = ctx_move(near0, lambda i: i + 2)
    near0_traded = swap(near0)
    near1 = jnp.where(last, traded0, after(near1, near0))
    far1 = ctx_move(near1, lambda i: i - 2)
    near1_traded = swap(near1)
    far0_traded = swap(far0)
    far1_traded = swap(far1)

    def facts(half):
        block = c if half == 0 else 2 * ctx_size - 1 - c
        info = jnp.stack([block * blk, core == half, last]).astype(jnp.int32)
        return info, query_heads, doc_start[half][:, None]

    w_peer = mirror(after(w_peer, far0))
    [mixed0] = attention(
        0, 1, *facts(0), kv0, traded0, near0, after(near0_traded, near1_traded), far0, far0_traded,
        near0, near0_traded,
    )
    kv1 = after(kv1, mixed0)
    mixed0 = after(mixed0, far1_traded, w_side, w_far)
    left, right, opposite = plus(mixed0), minus(mixed0), across(mixed0)
    [mixed1] = attention(
        1, 1, *facts(1), kv1, traded1, near1, near1_traded, far1, far1_traded, near0, near0_traded
    )
    peer = mirror(mixed1)
    piece = jax.ShapeDtypeStruct((blk, width), BF16)
    [part] = project(
        own_part_kernel, "own_part", [jax.ShapeDtypeStruct((ring, blk, width), F32)],
        [place, after(mixed1, left, right, opposite), out_weight], STEP,
    )
    w_peer2 = swap(after(w_peer, peer, part))
    far, up, down, keep1 = project(
        reduce_first_kernel, "reduce_first", [piece] * 4, [place, peer, part, w_peer, w_peer2]
    )
    got_far, got_up, got_down = across(far), plus(up), minus(down)
    w_side2, w_far2 = swap(after(w_side, far)), swap(after(w_far, far))
    send, keep0 = project(
        gather_first_kernel, "gather_first", [piece] * 2,
        [place, mixed0, left, right, opposite, out_weight, w_side, w_side2, w_far, w_far2],
    )
    got0 = mirror(send)
    [out1] = project(
        total_kernel, "total", [piece], [place, keep1, got_far, got_up, got_down], STEP
    )
    return project(
        finish_kernel, "finish", [jax.ShapeDtypeStruct((2, blk, width), BF16)],
        [place, keep0, got0, out1],
    )[0]


def solution(mesh):
    in_specs = (
        P(None, "ctx", "head"),
        P(None, "ctx", "head"),
        P(None, "ctx", "head"),
        P(None, "ctx"),
        P("head", None),
    )
    out_specs = P(None, "ctx", "head")
    return jax.shard_map(
        on_device, mesh=mesh, in_specs=in_specs, out_specs=out_specs, check_vma=False
    )
```

```python
import functools
import math

import jax
import jax.numpy as jnp
from jax import lax
from jax.experimental import pallas as pl
from jax.experimental.pallas import tpu as pltpu
from jax.sharding import PartitionSpec as P

HD = 128
LAGS = 4
TILE = 256
NEG = -1e30
NT = (((1,), (1,)), ((), ()))
NN = (((1,), (0,)), ((), ()))
VMEM = pl.BlockSpec(memory_space=pltpu.VMEM)
SMEM = pl.BlockSpec(memory_space=pltpu.SMEM)
STEP = 10**9
SMALL = pl.CostEstimate(flops=1, bytes_accessed=1, transcendentals=0)
F32 = jnp.float32
BF16 = jnp.bfloat16


def mm(a, b, dims=NN):
    return lax.dot_general(a, b, dims, preferred_element_type=F32)


def attn_kernel(
    half, info_ref, q_ref, doc_ref, own_ref, traded_ref, near_ref, near_traded_ref, far_ref,
    far_traded_ref, fold_near_ref, fold_traded_ref, *refs,
):
    *out_refs, kk, vv, sbuf = refs
    blk = own_ref.shape[1]
    heads = q_ref.shape[2] // HD
    base = info_ref[0]
    hard = info_ref[1] == 1
    easy = info_ref[1] == 0

    def fill(lag, ref):
        rows = pl.ds(lag * blk, blk)
        k = ref[0]
        kk[rows, :HD] = k
        kk[rows, HD:] = k
        vv[rows, :HD] = ref[1]
        vv[rows, HD:] = jnp.ones((blk, HD), BF16)

    def choose(lag, cases):
        for condition, ref in cases:
            pl.when(condition)(functools.partial(fill, lag, ref))

    fill(0, own_ref)
    fill(2, near_ref)
    choose(1, ((hard, near_traded_ref), (easy, traded_ref)))
    if half == 0:
        fill(4, far_ref)
        choose(3, ((hard, far_traded_ref), (easy, near_traded_ref)))
    else:
        folded = info_ref[2] == 1
        plain = info_ref[2] == 0
        choose(4, ((folded, fold_traded_ref), (plain, far_ref)))
        choose(3, (
            (jnp.logical_and(hard, plain), far_traded_ref),
            (jnp.logical_and(hard, folded), fold_near_ref),
            (easy, near_traded_ref),
        ))

    factor = HD ** -0.5 * math.log2(math.e)
    tiles = blk // TILE
    far = LAGS * blk
    for t in range(tiles):
        r0 = t * TILE
        rel = doc_ref[r0:r0 + TILE, :] - base
        col = lax.broadcasted_iota(jnp.int32, (TILE, blk), 1)
        row_t = lax.broadcasted_iota(jnp.int32, (TILE, TILE), 0)
        col_t = lax.broadcasted_iota(jnp.int32, (TILE, TILE), 1)
        tri = col_t <= row_t
        for a in range(heads):
            sb = sbuf.at[(t * heads + a) % 2]
            qf = q_ref[half, r0:r0 + TILE, a * HD:(a + 1) * HD].astype(F32) * factor
            hi = qf.astype(BF16)
            lo = (qf - hi.astype(F32)).astype(BF16)
            qq = jnp.concatenate([hi, lo], axis=1)

            def scores(first, count):
                return mm(qq, kk[first:first + count, :], NT)

            def running(m, s):
                for x in range(s.shape[1] // HD):
                    p = s[:, x * HD:(x + 1) * HD]
                    m = p if m is None else jnp.maximum(m, p)
                return m

            m = None
            pieces = []
            off = 0
            for lag in (3, 2, 1):
                s = jnp.where(col - lag * blk >= rel, scores(lag * blk, blk), NEG)
                m = running(m, s)
                sb[:, off:off + blk] = s
                pieces.append((off, blk, lag * blk))
                off += blk
            for u in range(tiles):
                if u == t:
                    continue
                lag = 0 if u < t else LAGS
                first = lag * blk + u * TILE
                s = jnp.where(col_t + (u * TILE - lag * blk) >= rel, scores(first, TILE), NEG)
                m = running(m, s)
                sb[:, off:off + TILE] = s
                pieces.append((off, TILE, first))
                off += TILE
            s = jnp.where(tri, scores(r0, TILE), scores(far + r0, TILE))
            position = jnp.where(tri, col_t + r0, col_t + (r0 - far))
            s = jnp.where(position >= rel, s, NEG)
            m = running(m, s)
            sb[:, off:off + TILE] = s
            top = jnp.max(m, axis=1, keepdims=True)
            acc = jnp.zeros((TILE, 2 * HD), F32)
            for begin, count, first in pieces:
                p = jnp.exp2(sb[:, begin:begin + count] - top).astype(BF16)
                acc = acc + mm(p, vv[first:first + count, :])
            p = jnp.exp2(sb[:, off:off + TILE] - top).astype(BF16)
            zero = jnp.zeros_like(p)
            acc = acc + mm(jnp.where(tri, p, zero), vv[r0:r0 + TILE, :])
            acc = acc + mm(jnp.where(tri, zero, p), vv[far + r0:far + r0 + TILE, :])
            result = (acc[:, :HD] / acc[:, HD:]).astype(BF16)
            count = out_refs[0].shape[0]
            out_refs[r0 // count][r0 % count:r0 % count + TILE, a * HD:(a + 1) * HD] = result


def attention(half, outs, info, q, doc, *blocks):
    _, rows, cols = q.shape
    keys = (LAGS + 1) * rows
    return pl.pallas_call(
        functools.partial(attn_kernel, half),
        out_shape=[jax.ShapeDtypeStruct((rows // outs, cols), BF16)] * outs,
        in_specs=[SMEM] + [VMEM] * (2 + len(blocks)),
        out_specs=[VMEM] * outs,
        scratch_shapes=[
            pltpu.VMEM((keys, 2 * HD), BF16),
            pltpu.VMEM((keys, 2 * HD), BF16),
            pltpu.VMEM((2, TILE, LAGS * rows), F32),
        ],
        compiler_params=pltpu.CompilerParams(vmem_limit_bytes=16 * 2**20),
        cost_estimate=pl.CostEstimate(flops=4 * 10**9, bytes_accessed=1, transcendentals=0) if half == 0 else pl.CostEstimate(
            flops=16 * rows * cols * keys, bytes_accessed=4 * 2**20,
            transcendentals=rows * cols // HD * keys,
        ),
        name="attend" + str(half),
    )(info, q, doc, *blocks)


def weights_kernel(info_ref, w_ref, side_ref, far_ref, peer_ref):
    x, y, core = info_ref[0], info_ref[1], info_ref[2]
    rows, wide = far_ref.shape
    width = wide // 2
    ring = peer_ref.shape[0] // rows
    mine = pl.ds(pl.multiple_of(core * rows, rows), rows)

    def columns(first, count):
        return pl.ds(pl.multiple_of(first * count, count), count)

    side_ref[...] = w_ref[:, columns(lax.rem(x + 1 + (ring - 2) * core, ring), wide)]
    far_ref[...] = w_ref[mine, columns(lax.rem(x + 2, ring), wide)]
    for i in range(ring):
        peer_ref[i * rows:(i + 1) * rows, :] = w_ref[mine, columns(2 * i + 1 - y, width)]


def split_weights(info, w, ring):
    rows, cols = w.shape
    return pl.pallas_call(
        weights_kernel,
        out_shape=[
            jax.ShapeDtypeStruct((rows, cols // ring), BF16),
            jax.ShapeDtypeStruct((rows // 2, cols // ring), BF16),
            jax.ShapeDtypeStruct((rows // 2 * ring, cols // ring // 2), BF16),
        ],
        in_specs=[SMEM, VMEM],
        out_specs=[VMEM] * 3,
        compiler_params=pltpu.CompilerParams(vmem_limit_bytes=16 * 2**20),
        cost_estimate=SMALL,
        name="split_weights",
    )(info, w)


def halves(core, rows):
    h = rows // 2
    return pl.ds(pl.multiple_of(core * h, h), h), pl.ds(pl.multiple_of((1 - core) * h, h), h)


def gather_first_kernel(
    info_ref, own_ref, left_ref, right_ref, far_ref, w_ref,
    ws_ref, wsp_ref, wf_ref, wfp_ref, send_ref, keep_ref,
):
    x, y, core = info_ref[0], info_ref[1], info_ref[2]
    rows, width = own_ref.shape
    mine, other = halves(core, width)
    cut = rows // 2

    def block(side, r):
        wide = pl.ds(pl.multiple_of(side * width, width), width)
        own_cols = pl.ds(pl.multiple_of((2 * x + side) * width, width), width)
        left, right = left_ref[r, :], right_ref[r, :]
        acc = mm(own_ref[r, :], w_ref[:, own_cols])
        acc = acc + mm(jnp.where(core == 0, left, right), ws_ref[:, wide])
        acc = acc + mm(jnp.where(core == 0, right, left), wsp_ref[:, wide])
        acc = acc + mm(far_ref[r, mine], wf_ref[:, wide])
        acc = acc + mm(far_ref[r, other], wfp_ref[:, wide])
        return acc.astype(BF16)

    for r in (slice(0, cut), slice(cut, rows)):
        send_ref[r, :] = block(1 - y, r)
    for r in (slice(0, cut), slice(cut, rows)):
        keep_ref[r, :] = block(y, r)


def targets(x, ring):
    return lax.rem(x + 2, ring), lax.rem(x + 1, ring), lax.rem(x + ring - 1, ring), x


def own_part_kernel(info_ref, own_ref, w_ref, part_ref):
    x, y = info_ref[0], info_ref[1]
    width = own_ref.shape[1]
    for i, target in enumerate(targets(x, part_ref.shape[0])):
        cols = pl.ds(pl.multiple_of((2 * target + y) * width, width), width)
        part_ref[i] = mm(own_ref[...], w_ref[:, cols])


def reduce_first_kernel(
    info_ref, peer_ref, part_ref, wm_ref, wp_ref, far_ref, up_ref, down_ref, keep_ref
):
    x, core = info_ref[0], info_ref[2]
    rows, width = peer_ref.shape
    mine, other = halves(core, width)
    h = width // 2
    ring = part_ref.shape[0]
    for i, (ref, target) in enumerate(
        zip((far_ref, up_ref, down_ref, keep_ref), targets(x, ring))
    ):
        w_rows = pl.ds(pl.multiple_of(target * h, h), h)
        for r in (slice(0, rows // 2), slice(rows // 2, rows)):
            acc = part_ref[i, r, :] + mm(peer_ref[r, mine], wm_ref[w_rows, :])
            ref[r, :] = (acc + mm(peer_ref[r, other], wp_ref[w_rows, :])).astype(BF16)


def total_kernel(info_ref, first_ref, *refs):
    *more, o_ref = refs
    total = first_ref[...].astype(F32)
    for ref in more:
        total = total + ref[...].astype(F32)
    o_ref[...] = total.astype(BF16)


def finish_kernel(info_ref, keep_ref, got_ref, done_ref, o_ref):
    o_ref[0] = (keep_ref[...].astype(F32) + got_ref[...].astype(F32)).astype(BF16)
    o_ref[1] = done_ref[...]


def project(kernel, name, outs, args, cost=0):
    return pl.pallas_call(
        kernel,
        out_shape=outs,
        in_specs=[SMEM] + [VMEM] * (len(args) - 1),
        out_specs=[VMEM] * len(outs),
        compiler_params=pltpu.CompilerParams(vmem_limit_bytes=16 * 2**20),
        cost_estimate=pl.CostEstimate(flops=cost, bytes_accessed=1, transcendentals=0),
        name=name,
    )(*args)


def after(array, *others):
    return lax.optimization_barrier((array, *others))[0]


def on_device(query_heads, key_heads, value_heads, doc_start, out_weight):
    ctx_size = lax.axis_size("ctx")
    c = lax.axis_index("ctx")
    head = lax.axis_index("head")
    core = c % 2
    x, y = head // 2, head % 2
    ring = lax.axis_size("head") // 2
    blk = key_heads.shape[1]
    width = query_heads.shape[2]

    def ctx_move(array, to):
        return lax.ppermute(
            array, "ctx", [(i, to(i)) for i in range(ctx_size) if 0 <= to(i) < ctx_size]
        )

    def head_move(array, to):
        return lax.ppermute(array, "head", [(i, to(i)) for i in range(2 * ring)])

    def swap(array):
        return ctx_move(array, lambda i: i ^ 1)

    def plus(array):
        return head_move(array, lambda i: (i + 2) % (2 * ring))

    def minus(array):
        return head_move(array, lambda i: (i - 2) % (2 * ring))

    def across(array):
        return head_move(array, lambda i: (i + 4) % (2 * ring))

    def mirror(array):
        return head_move(array, lambda i: i ^ 1)

    kv0 = jnp.stack([key_heads[0], value_heads[0]])
    kv1 = jnp.stack([key_heads[1], value_heads[1]])
    near0 = ctx_move(kv0, lambda i: i + 2)
    near1 = ctx_move(kv1, lambda i: i - 2)
    traded0 = swap(kv0)
    traded1 = swap(kv1)

    place = jnp.stack([x, y, core]).astype(jnp.int32)
    w_side, w_far, w_peer = split_weights(place, out_weight, ring)
    heads = 2 * ring
    w_side, w_far = after(w_side, traded0, traded1), after(w_far, traded0, traded1)
    w_side = lax.ppermute(w_side, ("ctx", "head"), [
        (i * heads + j, i * heads + (j + (2 if i % 2 == 0 else heads - 2)) % heads)
        for i in range(ctx_size) for j in range(heads)
    ])
    w_far = across(w_far)

    last = c >= ctx_size - 2
    near0 = after(near0, near1, traded0, traded1, w_peer)
    far0 = ctx_move(near0, lambda i: i + 2)
    near0_traded = swap(near0)
    near1 = jnp.where(last, traded0, after(near1, near0))
    far1 = ctx_move(near1, lambda i: i - 2)
    near1_traded = swap(near1)
    far0_traded = swap(far0)
    far1_traded = swap(far1)

    def facts(half):
        block = c if half == 0 else 2 * ctx_size - 1 - c
        info = jnp.stack([block * blk, core == half, last]).astype(jnp.int32)
        return info, query_heads, doc_start[half][:, None]

    w_peer = mirror(after(w_peer, far0))
    [mixed0] = attention(
        0, 1, *facts(0), kv0, traded0, near0, after(near0_traded, near1_traded), far0, far0_traded,
        near0, near0_traded,
    )
    kv1 = after(kv1, mixed0)
    mixed0 = after(mixed0, far1_traded, w_side, w_far)
    left, right, opposite = plus(mixed0), minus(mixed0), across(mixed0)
    [mixed1] = attention(
        1, 1, *facts(1), kv1, traded1, near1, near1_traded, far1, far1_traded, near0, near0_traded
    )
    peer = mirror(mixed1)
    piece = jax.ShapeDtypeStruct((blk, width), BF16)
    [part] = project(
        own_part_kernel, "own_part", [jax.ShapeDtypeStruct((ring, blk, width), F32)],
        [place, after(mixed1, left, right, opposite), out_weight], 8 * STEP,
    )
    w_peer2 = swap(after(w_peer, mixed1))
    far, up, down, keep1 = project(
        reduce_first_kernel, "reduce_first", [piece] * 4, [place, peer, part, w_peer, w_peer2]
    )
    got_far, got_up, got_down = across(far), plus(up), minus(down)
    w_side2, w_far2 = swap(after(w_side, far)), swap(after(w_far, far))
    send, keep0 = project(
        gather_first_kernel, "gather_first", [piece] * 2,
        [place, mixed0, left, right, opposite, out_weight, w_side, w_side2, w_far, w_far2],
    )
    got0 = mirror(send)
    [out1] = project(
        total_kernel, "total", [piece], [place, keep1, got_far, got_up, got_down], STEP
    )
    return project(
        finish_kernel, "finish", [jax.ShapeDtypeStruct((2, blk, width), BF16)],
        [place, keep0, got0, out1],
    )[0]


def solution(mesh):
    in_specs = (
        P(None, "ctx", "head"),
        P(None, "ctx", "head"),
        P(None, "ctx", "head"),
        P(None, "ctx"),
        P("head", None),
    )
    out_specs = P(None, "ctx", "head")
    return jax.shard_map(
        on_device, mesh=mesh, in_specs=in_specs, out_specs=out_specs, check_vma=False
    )
```

```python
import functools
import math

import jax
import jax.numpy as jnp
from jax import lax
from jax.experimental import pallas as pl
from jax.experimental.pallas import tpu as pltpu
from jax.sharding import PartitionSpec as P

HD = 128
LAGS = 4
TILE = 256
NEG = -1e30
NT = (((1,), (1,)), ((), ()))
NN = (((1,), (0,)), ((), ()))
VMEM = pl.BlockSpec(memory_space=pltpu.VMEM)
SMEM = pl.BlockSpec(memory_space=pltpu.SMEM)
STEP = 10**9
SMALL = pl.CostEstimate(flops=1, bytes_accessed=1, transcendentals=0)
F32 = jnp.float32
BF16 = jnp.bfloat16


def mm(a, b, dims=NN):
    return lax.dot_general(a, b, dims, preferred_element_type=F32)


def attn_kernel(
    half, info_ref, q_ref, doc_ref, own_ref, traded_ref, near_ref, near_traded_ref, far_ref,
    far_traded_ref, fold_near_ref, fold_traded_ref, *refs,
):
    *out_refs, kk, vv, sbuf = refs
    blk = own_ref.shape[1]
    heads = q_ref.shape[2] // HD
    base = info_ref[0]
    hard = info_ref[1] == 1
    easy = info_ref[1] == 0

    def fill(lag, ref):
        rows = pl.ds(lag * blk, blk)
        k = ref[0]
        kk[rows, :] = k
        vv[rows, :HD] = ref[1]
        vv[rows, HD:] = jnp.ones((blk, HD), BF16)

    def choose(lag, cases):
        for condition, ref in cases:
            pl.when(condition)(functools.partial(fill, lag, ref))

    fill(0, own_ref)
    fill(2, near_ref)
    choose(1, ((hard, near_traded_ref), (easy, traded_ref)))
    if half == 0:
        fill(4, far_ref)
        choose(3, ((hard, far_traded_ref), (easy, near_traded_ref)))
    else:
        folded = info_ref[2] == 1
        plain = info_ref[2] == 0
        choose(4, ((folded, fold_traded_ref), (plain, far_ref)))
        choose(3, (
            (jnp.logical_and(hard, plain), far_traded_ref),
            (jnp.logical_and(hard, folded), fold_near_ref),
            (easy, near_traded_ref),
        ))

    factor = HD ** -0.5 * math.log2(math.e)
    tiles = blk // TILE
    far = LAGS * blk
    col = lax.broadcasted_iota(jnp.int32, (TILE, blk), 1)
    row_t = lax.broadcasted_iota(jnp.int32, (TILE, TILE), 0)
    col_t = lax.broadcasted_iota(jnp.int32, (TILE, TILE), 1)
    tri = col_t <= row_t

    def unit(t, a, sb):
        r0 = t * TILE
        cols = slice(a * HD, (a + 1) * HD)
        rel = doc_ref[r0:r0 + TILE, :] - base
        q = q_ref[half, r0:r0 + TILE, cols]
        state = {"m": None, "acc": jnp.zeros((TILE, 2 * HD), F32)}

        def scores(first, count):
            return mm(q, kk[first:first + count, :], NT) * factor

        def keep(s, off):
            for x in range(s.shape[1] // HD):
                p = s[:, x * HD:(x + 1) * HD]
                state["m"] = p if state["m"] is None else jnp.maximum(state["m"], p)
            sb[:, off:off + s.shape[1]] = s

        def whole(lag, off):
            keep(jnp.where(col - lag * blk >= rel, scores(lag * blk, blk), NEG), off)

        def part(lag, u, off):
            s = scores(lag * blk + u * TILE, TILE)
            keep(jnp.where(col_t + (u * TILE - lag * blk) >= rel, s, NEG), off)

        def corner(off):
            s = jnp.where(tri, scores(r0, TILE), scores(far + r0, TILE))
            position = jnp.where(tri, col_t + r0, col_t + (r0 - far))
            keep(jnp.where(position >= rel, s, NEG), off)

        def mix(begin, count, first):
            p = jnp.exp2(sb[:, begin:begin + count] - state["top"]).astype(BF16)
            state["acc"] = state["acc"] + mm(p, vv[first:first + count, :])

        def mix_corner(off):
            p = jnp.exp2(sb[:, off:off + TILE] - state["top"]).astype(BF16)
            zero = jnp.zeros_like(p)
            acc = state["acc"] + mm(jnp.where(tri, p, zero), vv[r0:r0 + TILE, :])
            state["acc"] = acc + mm(jnp.where(tri, zero, p), vv[far + r0:far + r0 + TILE, :])

        def highest():
            state["top"] = jnp.max(state["m"], axis=1, keepdims=True)

        def store():
            acc = state["acc"]
            result = (acc[:, :HD] / acc[:, HD:]).astype(BF16)
            count = out_refs[0].shape[0]
            out_refs[r0 // count][r0 % count:r0 % count + TILE, cols] = result

        first_pass, second_pass = [], []
        off = 0
        for lag in (3, 2, 1):
            first_pass.append(functools.partial(whole, lag, off))
            second_pass.append(functools.partial(mix, off, blk, lag * blk))
            off += blk
        for u in range(tiles):
            if u != t:
                lag = 0 if u < t else LAGS
                first_pass.append(functools.partial(part, lag, u, off))
                second_pass.append(functools.partial(mix, off, TILE, lag * blk + u * TILE))
                off += TILE
        first_pass.append(functools.partial(corner, off))
        second_pass.append(functools.partial(mix_corner, off))
        return first_pass, highest, second_pass, store

    units = [
        unit(t, a, sbuf.at[(t * heads + a) % 2]) for t in range(tiles) for a in range(heads)
    ]
    for step in units[0][0]:
        step()
    units[0][1]()
    for i, (_, _, second_pass, store) in enumerate(units):
        following = units[i + 1][0] if i + 1 < len(units) else []
        for j in range(max(len(following), len(second_pass))):
            if j < len(following):
                following[j]()
            if j < len(second_pass):
                second_pass[j]()
        store()
        if following:
            units[i + 1][1]()


def attention(half, outs, info, q, doc, *blocks):
    _, rows, cols = q.shape
    keys = (LAGS + 1) * rows
    return pl.pallas_call(
        functools.partial(attn_kernel, half),
        out_shape=[jax.ShapeDtypeStruct((rows // outs, cols), BF16)] * outs,
        in_specs=[SMEM] + [VMEM] * (2 + len(blocks)),
        out_specs=[VMEM] * outs,
        scratch_shapes=[
            pltpu.VMEM((keys, HD), BF16),
            pltpu.VMEM((keys, 2 * HD), BF16),
            pltpu.VMEM((2, TILE, LAGS * rows), F32),
        ],
        compiler_params=pltpu.CompilerParams(vmem_limit_bytes=16 * 2**20),
        cost_estimate=pl.CostEstimate(flops=4 * 10**9, bytes_accessed=1, transcendentals=0) if half == 0 else pl.CostEstimate(
            flops=16 * rows * cols * keys, bytes_accessed=4 * 2**20,
            transcendentals=rows * cols // HD * keys,
        ),
        name="attend" + str(half),
    )(info, q, doc, *blocks)


def weights_kernel(info_ref, w_ref, side_ref, far_ref, peer_ref):
    x, y, core = info_ref[0], info_ref[1], info_ref[2]
    rows, wide = far_ref.shape
    width = wide // 2
    ring = peer_ref.shape[0] // rows
    mine = pl.ds(pl.multiple_of(core * rows, rows), rows)

    def columns(first, count):
        return pl.ds(pl.multiple_of(first * count, count), count)

    side_ref[...] = w_ref[:, columns(lax.rem(x + 1 + (ring - 2) * core, ring), wide)]
    far_ref[...] = w_ref[mine, columns(lax.rem(x + 2, ring), wide)]
    for i in range(ring):
        peer_ref[i * rows:(i + 1) * rows, :] = w_ref[mine, columns(2 * i + 1 - y, width)]


def split_weights(info, w, ring):
    rows, cols = w.shape
    return pl.pallas_call(
        weights_kernel,
        out_shape=[
            jax.ShapeDtypeStruct((rows, cols // ring), BF16),
            jax.ShapeDtypeStruct((rows // 2, cols // ring), BF16),
            jax.ShapeDtypeStruct((rows // 2 * ring, cols // ring // 2), BF16),
        ],
        in_specs=[SMEM, VMEM],
        out_specs=[VMEM] * 3,
        compiler_params=pltpu.CompilerParams(vmem_limit_bytes=16 * 2**20),
        cost_estimate=SMALL,
        name="split_weights",
    )(info, w)


def halves(core, rows):
    h = rows // 2
    return pl.ds(pl.multiple_of(core * h, h), h), pl.ds(pl.multiple_of((1 - core) * h, h), h)


def gather_first_kernel(
    info_ref, own_ref, left_ref, right_ref, far_ref, w_ref,
    ws_ref, wsp_ref, wf_ref, wfp_ref, send_ref, keep_ref,
):
    x, y, core = info_ref[0], info_ref[1], info_ref[2]
    rows, width = own_ref.shape
    mine, other = halves(core, width)
    cut = rows // 2

    def block(side, r):
        wide = pl.ds(pl.multiple_of(side * width, width), width)
        own_cols = pl.ds(pl.multiple_of((2 * x + side) * width, width), width)
        left, right = left_ref[r, :], right_ref[r, :]
        acc = mm(own_ref[r, :], w_ref[:, own_cols])
        acc = acc + mm(jnp.where(core == 0, left, right), ws_ref[:, wide])
        acc = acc + mm(jnp.where(core == 0, right, left), wsp_ref[:, wide])
        acc = acc + mm(far_ref[r, mine], wf_ref[:, wide])
        acc = acc + mm(far_ref[r, other], wfp_ref[:, wide])
        return acc.astype(BF16)

    for r in (slice(0, cut), slice(cut, rows)):
        send_ref[r, :] = block(1 - y, r)
    for r in (slice(0, cut), slice(cut, rows)):
        keep_ref[r, :] = block(y, r)


def targets(x, ring):
    return lax.rem(x + 2, ring), lax.rem(x + 1, ring), lax.rem(x + ring - 1, ring), x


def own_part_kernel(info_ref, own_ref, w_ref, part_ref):
    x, y = info_ref[0], info_ref[1]
    width = own_ref.shape[1]
    for i, target in enumerate(targets(x, part_ref.shape[0])):
        cols = pl.ds(pl.multiple_of((2 * target + y) * width, width), width)
        part_ref[i] = mm(own_ref[...], w_ref[:, cols])


def reduce_first_kernel(
    info_ref, peer_ref, part_ref, wm_ref, wp_ref, far_ref, up_ref, down_ref, keep_ref
):
    x, core = info_ref[0], info_ref[2]
    rows, width = peer_ref.shape
    mine, other = halves(core, width)
    h = width // 2
    ring = part_ref.shape[0]
    for i, (ref, target) in enumerate(
        zip((far_ref, up_ref, down_ref, keep_ref), targets(x, ring))
    ):
        w_rows = pl.ds(pl.multiple_of(target * h, h), h)
        for r in (slice(0, rows // 2), slice(rows // 2, rows)):
            acc = part_ref[i, r, :] + mm(peer_ref[r, mine], wm_ref[w_rows, :])
            ref[r, :] = (acc + mm(peer_ref[r, other], wp_ref[w_rows, :])).astype(BF16)


def total_kernel(info_ref, first_ref, *refs):
    *more, o_ref = refs
    total = first_ref[...].astype(F32)
    for ref in more:
        total = total + ref[...].astype(F32)
    o_ref[...] = total.astype(BF16)


def finish_kernel(info_ref, keep_ref, got_ref, done_ref, o_ref):
    o_ref[0] = (keep_ref[...].astype(F32) + got_ref[...].astype(F32)).astype(BF16)
    o_ref[1] = done_ref[...]


def project(kernel, name, outs, args, cost=0):
    return pl.pallas_call(
        kernel,
        out_shape=outs,
        in_specs=[SMEM] + [VMEM] * (len(args) - 1),
        out_specs=[VMEM] * len(outs),
        compiler_params=pltpu.CompilerParams(vmem_limit_bytes=16 * 2**20),
        cost_estimate=pl.CostEstimate(flops=cost, bytes_accessed=1, transcendentals=0),
        name=name,
    )(*args)


def after(array, *others):
    return lax.optimization_barrier((array, *others))[0]


def on_device(query_heads, key_heads, value_heads, doc_start, out_weight):
    ctx_size = lax.axis_size("ctx")
    c = lax.axis_index("ctx")
    head = lax.axis_index("head")
    core = c % 2
    x, y = head // 2, head % 2
    ring = lax.axis_size("head") // 2
    blk = key_heads.shape[1]
    width = query_heads.shape[2]

    def ctx_move(array, to):
        return lax.ppermute(
            array, "ctx", [(i, to(i)) for i in range(ctx_size) if 0 <= to(i) < ctx_size]
        )

    def head_move(array, to):
        return lax.ppermute(array, "head", [(i, to(i)) for i in range(2 * ring)])

    def swap(array):
        return ctx_move(array, lambda i: i ^ 1)

    def plus(array):
        return head_move(array, lambda i: (i + 2) % (2 * ring))

    def minus(array):
        return head_move(array, lambda i: (i - 2) % (2 * ring))

    def across(array):
        return head_move(array, lambda i: (i + 4) % (2 * ring))

    def mirror(array):
        return head_move(array, lambda i: i ^ 1)

    kv0 = jnp.stack([key_heads[0], value_heads[0]])
    kv1 = jnp.stack([key_heads[1], value_heads[1]])
    near0 = ctx_move(kv0, lambda i: i + 2)
    near1 = ctx_move(kv1, lambda i: i - 2)
    traded0 = swap(kv0)
    traded1 = swap(kv1)

    place = jnp.stack([x, y, core]).astype(jnp.int32)
    w_side, w_far, w_peer = split_weights(place, out_weight, ring)
    heads = 2 * ring
    w_side, w_far = after(w_side, traded0, traded1), after(w_far, traded0, traded1)
    w_side = lax.ppermute(w_side, ("ctx", "head"), [
        (i * heads + j, i * heads + (j + (2 if i % 2 == 0 else heads - 2)) % heads)
        for i in range(ctx_size) for j in range(heads)
    ])
    w_far = across(w_far)

    last = c >= ctx_size - 2
    near0 = after(near0, near1, traded0, traded1, w_peer)
    far0 = ctx_move(near0, lambda i: i + 2)
    near0_traded = swap(near0)
    near1 = jnp.where(last, traded0, after(near1, near0))
    far1 = ctx_move(near1, lambda i: i - 2)
    near1_traded = swap(near1)
    far0_traded = swap(far0)
    far1_traded = swap(far1)

    def facts(half):
        block = c if half == 0 else 2 * ctx_size - 1 - c
        info = jnp.stack([block * blk, core == half, last]).astype(jnp.int32)
        return info, query_heads, doc_start[half][:, None]

    w_peer = mirror(after(w_peer, far0))
    [mixed0] = attention(
        0, 1, *facts(0), kv0, traded0, near0, after(near0_traded, near1_traded), far0, far0_traded,
        near0, near0_traded,
    )
    kv1 = after(kv1, mixed0)
    mixed0 = after(mixed0, far1_traded, w_side, w_far)
    left, right, opposite = plus(mixed0), minus(mixed0), across(mixed0)
    [mixed1] = attention(
        1, 1, *facts(1), kv1, traded1, near1, near1_traded, far1, far1_traded, near0, near0_traded
    )
    peer = mirror(mixed1)
    piece = jax.ShapeDtypeStruct((blk, width), BF16)
    [part] = project(
        own_part_kernel, "own_part", [jax.ShapeDtypeStruct((ring, blk, width), F32)],
        [place, after(mixed1, left, right, opposite), out_weight], 8 * STEP,
    )
    w_peer2 = swap(after(w_peer, mixed1))
    far, up, down, keep1 = project(
        reduce_first_kernel, "reduce_first", [piece] * 4, [place, peer, part, w_peer, w_peer2]
    )
    got_far, got_up, got_down = across(far), plus(up), minus(down)
    w_side2, w_far2 = swap(after(w_side, far)), swap(after(w_far, far))
    send, keep0 = project(
        gather_first_kernel, "gather_first", [piece] * 2,
        [place, mixed0, left, right, opposite, out_weight, w_side, w_side2, w_far, w_far2],
    )
    got0 = mirror(send)
    [out1] = project(
        total_kernel, "total", [piece], [place, keep1, got_far, got_up, got_down], STEP
    )
    return project(
        finish_kernel, "finish", [jax.ShapeDtypeStruct((2, blk, width), BF16)],
        [place, keep0, got0, out1],
    )[0]


def solution(mesh):
    in_specs = (
        P(None, "ctx", "head"),
        P(None, "ctx", "head"),
        P(None, "ctx", "head"),
        P(None, "ctx"),
        P("head", None),
    )
    out_specs = P(None, "ctx", "head")
    return jax.shard_map(
        on_device, mesh=mesh, in_specs=in_specs, out_specs=out_specs, check_vma=False
    )
```

```python
import functools
import math

import jax
import jax.numpy as jnp
from jax import lax
from jax.experimental import pallas as pl
from jax.experimental.pallas import tpu as pltpu
from jax.sharding import PartitionSpec as P

HD = 128
LAGS = 4
TILE = 256
NEG = -1e30
NT = (((1,), (1,)), ((), ()))
NN = (((1,), (0,)), ((), ()))
VMEM = pl.BlockSpec(memory_space=pltpu.VMEM)
SMEM = pl.BlockSpec(memory_space=pltpu.SMEM)
STEP = 10**9
SMALL = pl.CostEstimate(flops=1, bytes_accessed=1, transcendentals=0)
F32 = jnp.float32
BF16 = jnp.bfloat16


def mm(a, b, dims=NN):
    return lax.dot_general(a, b, dims, preferred_element_type=F32)


def attn_kernel(
    half, info_ref, q_ref, doc_ref, own_ref, traded_ref, near_ref, near_traded_ref, far_ref,
    far_traded_ref, fold_near_ref, fold_traded_ref, *refs,
):
    *out_refs, kk, vv, sbuf = refs
    blk = own_ref.shape[1]
    heads = q_ref.shape[2] // HD
    base = info_ref[0]
    hard = info_ref[1] == 1
    easy = info_ref[1] == 0

    def fill(lag, ref):
        rows = pl.ds(lag * blk, blk)
        k = ref[0]
        kk[rows, :] = k
        vv[rows, :HD] = ref[1]
        vv[rows, HD:] = jnp.ones((blk, HD), BF16)

    def choose(lag, cases):
        for condition, ref in cases:
            pl.when(condition)(functools.partial(fill, lag, ref))

    fill(0, own_ref)
    fill(2, near_ref)
    choose(1, ((hard, near_traded_ref), (easy, traded_ref)))
    if half == 0:
        fill(4, far_ref)
        choose(3, ((hard, far_traded_ref), (easy, near_traded_ref)))
    else:
        folded = info_ref[2] == 1
        plain = info_ref[2] == 0
        choose(4, ((folded, fold_traded_ref), (plain, far_ref)))
        choose(3, (
            (jnp.logical_and(hard, plain), far_traded_ref),
            (jnp.logical_and(hard, folded), fold_near_ref),
            (easy, near_traded_ref),
        ))

    factor = HD ** -0.5 * math.log2(math.e)
    tiles = blk // TILE
    far = LAGS * blk
    col = lax.broadcasted_iota(jnp.int32, (TILE, blk), 1)
    row_t = lax.broadcasted_iota(jnp.int32, (TILE, TILE), 0)
    col_t = lax.broadcasted_iota(jnp.int32, (TILE, TILE), 1)
    tri = col_t <= row_t

    def unit(t, a, sb):
        r0 = t * TILE
        cols = slice(a * HD, (a + 1) * HD)
        rel = doc_ref[r0:r0 + TILE, :] - base
        q = q_ref[half, r0:r0 + TILE, cols]
        state = {"m": None, "acc": jnp.zeros((TILE, 2 * HD), F32)}

        def scores(first, count):
            return mm(q, kk[first:first + count, :], NT) * factor

        def keep(s, off):
            for x in range(s.shape[1] // HD):
                p = s[:, x * HD:(x + 1) * HD]
                state["m"] = p if state["m"] is None else jnp.maximum(state["m"], p)
            sb[:, off:off + s.shape[1]] = s

        def whole(lag, off):
            keep(jnp.where(col - lag * blk >= rel, scores(lag * blk, blk), NEG), off)

        def part(lag, u, off):
            s = scores(lag * blk + u * TILE, TILE)
            keep(jnp.where(col_t + (u * TILE - lag * blk) >= rel, s, NEG), off)

        def corner(off):
            s = jnp.where(tri, scores(r0, TILE), scores(far + r0, TILE))
            position = jnp.where(tri, col_t + r0, col_t + (r0 - far))
            keep(jnp.where(position >= rel, s, NEG), off)

        def mix(begin, count, first):
            p = jnp.exp2(sb[:, begin:begin + count] - state["top"]).astype(BF16)
            state["acc"] = state["acc"] + mm(p, vv[first:first + count, :])

        def mix_corner(off):
            p = jnp.exp2(sb[:, off:off + TILE] - state["top"]).astype(BF16)
            zero = jnp.zeros_like(p)
            acc = state["acc"] + mm(jnp.where(tri, p, zero), vv[r0:r0 + TILE, :])
            state["acc"] = acc + mm(jnp.where(tri, zero, p), vv[far + r0:far + r0 + TILE, :])

        def highest():
            state["top"] = jnp.max(state["m"], axis=1, keepdims=True)

        def store():
            acc = state["acc"]
            result = (acc[:, :HD] / acc[:, HD:]).astype(BF16)
            count = out_refs[0].shape[0]
            out_refs[r0 // count][r0 % count:r0 % count + TILE, cols] = result

        first_pass, second_pass = [], []
        off = 0
        for lag in (3, 2, 1):
            first_pass.append(functools.partial(whole, lag, off))
            second_pass.append(functools.partial(mix, off, blk, lag * blk))
            off += blk
        for u in range(tiles):
            if u != t:
                lag = 0 if u < t else LAGS
                first_pass.append(functools.partial(part, lag, u, off))
                second_pass.append(functools.partial(mix, off, TILE, lag * blk + u * TILE))
                off += TILE
        first_pass.append(functools.partial(corner, off))
        second_pass.append(functools.partial(mix_corner, off))
        return first_pass, highest, second_pass, store

    units = [
        unit(t, a, sbuf.at[(t * heads + a) % 2]) for t in range(tiles) for a in range(heads)
    ]
    for step in units[0][0]:
        step()
    units[0][1]()
    for i, (_, _, second_pass, store) in enumerate(units):
        following = units[i + 1][0] if i + 1 < len(units) else []
        for j in range(max(len(following), len(second_pass))):
            if j < len(following):
                following[j]()
            if j < len(second_pass):
                second_pass[j]()
        store()
        if following:
            units[i + 1][1]()


def attention(half, outs, info, q, doc, *blocks):
    _, rows, cols = q.shape
    keys = (LAGS + 1) * rows
    return pl.pallas_call(
        functools.partial(attn_kernel, half),
        out_shape=[jax.ShapeDtypeStruct((rows // outs, cols), BF16)] * outs,
        in_specs=[SMEM] + [VMEM] * (2 + len(blocks)),
        out_specs=[VMEM] * outs,
        scratch_shapes=[
            pltpu.VMEM((keys, HD), BF16),
            pltpu.VMEM((keys, 2 * HD), BF16),
            pltpu.VMEM((2, TILE, LAGS * rows), F32),
        ],
        compiler_params=pltpu.CompilerParams(vmem_limit_bytes=16 * 2**20),
        cost_estimate=pl.CostEstimate(flops=4 * 10**9, bytes_accessed=1, transcendentals=0) if half == 0 else pl.CostEstimate(
            flops=16 * rows * cols * keys, bytes_accessed=4 * 2**20,
            transcendentals=rows * cols // HD * keys,
        ),
        name="attend" + str(half),
    )(info, q, doc, *blocks)


def weights_kernel(info_ref, w_ref, side_ref, far_ref, peer_ref):
    x, y, core = info_ref[0], info_ref[1], info_ref[2]
    rows, wide = far_ref.shape
    width = wide // 2
    ring = peer_ref.shape[0] // rows
    mine = pl.ds(pl.multiple_of(core * rows, rows), rows)

    def columns(first, count):
        return pl.ds(pl.multiple_of(first * count, count), count)

    side_ref[...] = w_ref[:, columns(lax.rem(x + 1 + (ring - 2) * core, ring), wide)]
    far_ref[...] = w_ref[mine, columns(lax.rem(x + 2, ring), wide)]
    for i in range(ring):
        peer_ref[i * rows:(i + 1) * rows, :] = w_ref[mine, columns(2 * i + 1 - y, width)]


def split_weights(info, w, ring):
    rows, cols = w.shape
    return pl.pallas_call(
        weights_kernel,
        out_shape=[
            jax.ShapeDtypeStruct((rows, cols // ring), BF16),
            jax.ShapeDtypeStruct((rows // 2, cols // ring), BF16),
            jax.ShapeDtypeStruct((rows // 2 * ring, cols // ring // 2), BF16),
        ],
        in_specs=[SMEM, VMEM],
        out_specs=[VMEM] * 3,
        compiler_params=pltpu.CompilerParams(vmem_limit_bytes=16 * 2**20),
        cost_estimate=SMALL,
        name="split_weights",
    )(info, w)


def halves(core, rows):
    h = rows // 2
    return pl.ds(pl.multiple_of(core * h, h), h), pl.ds(pl.multiple_of((1 - core) * h, h), h)


def gather_first_kernel(
    info_ref, own_ref, left_ref, right_ref, far_ref, w_ref,
    ws_ref, wsp_ref, wf_ref, wfp_ref, send_ref, keep_ref,
):
    x, y, core = info_ref[0], info_ref[1], info_ref[2]
    rows, width = own_ref.shape
    mine, other = halves(core, width)
    cut = rows // 2

    def block(side, r):
        wide = pl.ds(pl.multiple_of(side * width, width), width)
        own_cols = pl.ds(pl.multiple_of((2 * x + side) * width, width), width)
        left, right = left_ref[r, :], right_ref[r, :]
        acc = mm(own_ref[r, :], w_ref[:, own_cols])
        acc = acc + mm(jnp.where(core == 0, left, right), ws_ref[:, wide])
        acc = acc + mm(jnp.where(core == 0, right, left), wsp_ref[:, wide])
        acc = acc + mm(far_ref[r, mine], wf_ref[:, wide])
        acc = acc + mm(far_ref[r, other], wfp_ref[:, wide])
        return acc.astype(BF16)

    for r in (slice(0, cut), slice(cut, rows)):
        send_ref[r, :] = block(1 - y, r)
    for r in (slice(0, cut), slice(cut, rows)):
        keep_ref[r, :] = block(y, r)


def targets(x, ring):
    return lax.rem(x + 2, ring), lax.rem(x + 1, ring), lax.rem(x + ring - 1, ring), x


def own_part_kernel(info_ref, own_ref, w_ref, part_ref):
    x, y = info_ref[0], info_ref[1]
    width = own_ref.shape[1]
    for i, target in enumerate(targets(x, part_ref.shape[0])):
        cols = pl.ds(pl.multiple_of((2 * target + y) * width, width), width)
        part_ref[i] = mm(own_ref[...], w_ref[:, cols])


def reduce_first_kernel(
    info_ref, peer_ref, part_ref, wm_ref, wp_ref, far_ref, up_ref, down_ref, keep_ref
):
    x, core = info_ref[0], info_ref[2]
    rows, width = peer_ref.shape
    mine, other = halves(core, width)
    h = width // 2
    ring = part_ref.shape[0]
    for i, (ref, target) in enumerate(
        zip((far_ref, up_ref, down_ref, keep_ref), targets(x, ring))
    ):
        w_rows = pl.ds(pl.multiple_of(target * h, h), h)
        for r in (slice(0, rows // 2), slice(rows // 2, rows)):
            acc = part_ref[i, r, :] + mm(peer_ref[r, mine], wm_ref[w_rows, :])
            ref[r, :] = (acc + mm(peer_ref[r, other], wp_ref[w_rows, :])).astype(BF16)


def order_kernel(info_ref, o_ref):
    for i in range(3):
        o_ref[i] = info_ref[i]


def total_kernel(info_ref, first_ref, *refs):
    *more, o_ref = refs
    total = first_ref[...].astype(F32)
    for ref in more:
        total = total + ref[...].astype(F32)
    o_ref[...] = total.astype(BF16)


def finish_kernel(info_ref, keep_ref, got_ref, done_ref, o_ref):
    o_ref[0] = (keep_ref[...].astype(F32) + got_ref[...].astype(F32)).astype(BF16)
    o_ref[1] = done_ref[...]


def project(kernel, name, outs, args, cost=0):
    return pl.pallas_call(
        kernel,
        out_shape=outs,
        in_specs=[SMEM] + [VMEM] * (len(args) - 1),
        out_specs=[VMEM] * len(outs),
        compiler_params=pltpu.CompilerParams(vmem_limit_bytes=16 * 2**20),
        cost_estimate=pl.CostEstimate(flops=cost, bytes_accessed=1, transcendentals=0),
        name=name,
    )(*args)


def after(array, *others):
    return lax.optimization_barrier((array, *others))[0]


def on_device(query_heads, key_heads, value_heads, doc_start, out_weight):
    ctx_size = lax.axis_size("ctx")
    c = lax.axis_index("ctx")
    head = lax.axis_index("head")
    core = c % 2
    x, y = head // 2, head % 2
    ring = lax.axis_size("head") // 2
    blk = key_heads.shape[1]
    width = query_heads.shape[2]

    def ctx_move(array, to):
        return lax.ppermute(
            array, "ctx", [(i, to(i)) for i in range(ctx_size) if 0 <= to(i) < ctx_size]
        )

    def head_move(array, to):
        return lax.ppermute(array, "head", [(i, to(i)) for i in range(2 * ring)])

    def swap(array):
        return ctx_move(array, lambda i: i ^ 1)

    def plus(array):
        return head_move(array, lambda i: (i + 2) % (2 * ring))

    def minus(array):
        return head_move(array, lambda i: (i - 2) % (2 * ring))

    def across(array):
        return head_move(array, lambda i: (i + 4) % (2 * ring))

    def mirror(array):
        return head_move(array, lambda i: i ^ 1)

    kv0 = jnp.stack([key_heads[0], value_heads[0]])
    kv1 = jnp.stack([key_heads[1], value_heads[1]])
    near0 = ctx_move(kv0, lambda i: i + 2)
    near1 = ctx_move(kv1, lambda i: i - 2)
    traded0 = swap(kv0)
    traded1 = swap(kv1)

    place = jnp.stack([x, y, core]).astype(jnp.int32)
    w_side, w_far, w_peer = split_weights(place, out_weight, ring)
    heads = 2 * ring
    w_side, w_far = after(w_side, traded0, traded1), after(w_far, traded0, traded1)
    w_side = lax.ppermute(w_side, ("ctx", "head"), [
        (i * heads + j, i * heads + (j + (2 if i % 2 == 0 else heads - 2)) % heads)
        for i in range(ctx_size) for j in range(heads)
    ])
    w_far = across(w_far)

    last = c >= ctx_size - 2
    near0 = after(near0, near1, traded0, traded1, w_peer)
    far0 = ctx_move(near0, lambda i: i + 2)
    near0_traded = swap(near0)
    near1 = jnp.where(last, traded0, after(near1, near0))
    far1 = ctx_move(near1, lambda i: i - 2)
    near1_traded = swap(near1)
    far0_traded = swap(far0)
    far1_traded = swap(far1)

    def facts(half):
        block = c if half == 0 else 2 * ctx_size - 1 - c
        info = jnp.stack([block * blk, core == half, last]).astype(jnp.int32)
        return info, query_heads, doc_start[half][:, None]

    w_peer = mirror(after(w_peer, far0))
    [mixed0] = attention(
        0, 1, *facts(0), kv0, traded0, near0, after(near0_traded, near1_traded), far0, far0_traded,
        near0, near0_traded,
    )
    kv1 = after(kv1, mixed0)
    mixed0 = after(mixed0, far1_traded, w_side, w_far)
    left, right, opposite = plus(mixed0), minus(mixed0), across(mixed0)
    [mixed1] = attention(
        1, 1, *facts(1), kv1, traded1, near1, near1_traded, far1, far1_traded, near0, near0_traded
    )
    peer = mirror(mixed1)
    piece = jax.ShapeDtypeStruct((blk, width), BF16)
    [part] = project(
        own_part_kernel, "own_part", [jax.ShapeDtypeStruct((ring, blk, width), F32)],
        [place, mixed1, out_weight],
    )
    w_peer2 = swap(after(w_peer, mixed1))
    gathered_place = pl.pallas_call(
        order_kernel,
        out_shape=jax.ShapeDtypeStruct((3,), jnp.int32),
        in_specs=[SMEM],
        out_specs=SMEM,
        compiler_params=pltpu.CompilerParams(vmem_limit_bytes=16 * 2**20),
        cost_estimate=pl.CostEstimate(flops=8 * STEP, bytes_accessed=1, transcendentals=0),
        name="order",
    )(after(place, left, right, opposite, part))
    far, up, down, keep1 = project(
        reduce_first_kernel, "reduce_first", [piece] * 4, [gathered_place, peer, part, w_peer, w_peer2]
    )
    got_far, got_up, got_down = across(far), plus(up), minus(down)
    w_side2, w_far2 = swap(after(w_side, far)), swap(after(w_far, far))
    send, keep0 = project(
        gather_first_kernel, "gather_first", [piece] * 2,
        [place, mixed0, left, right, opposite, out_weight, w_side, w_side2, w_far, w_far2],
    )
    got0 = mirror(send)
    [out1] = project(
        total_kernel, "total", [piece], [place, keep1, got_far, got_up, got_down], STEP
    )
    return project(
        finish_kernel, "finish", [jax.ShapeDtypeStruct((2, blk, width), BF16)],
        [place, keep0, got0, out1],
    )[0]


def solution(mesh):
    in_specs = (
        P(None, "ctx", "head"),
        P(None, "ctx", "head"),
        P(None, "ctx", "head"),
        P(None, "ctx"),
        P("head", None),
    )
    out_specs = P(None, "ctx", "head")
    return jax.shard_map(
        on_device, mesh=mesh, in_specs=in_specs, out_specs=out_specs, check_vma=False
    )
```

```python
import functools
import math

import jax
import jax.numpy as jnp
from jax import lax
from jax.experimental import pallas as pl
from jax.experimental.pallas import tpu as pltpu
from jax.sharding import PartitionSpec as P

HD = 128
LAGS = 4
TILE = 256
NEG = -1e30
NT = (((1,), (1,)), ((), ()))
NN = (((1,), (0,)), ((), ()))
VMEM = pl.BlockSpec(memory_space=pltpu.VMEM)
SMEM = pl.BlockSpec(memory_space=pltpu.SMEM)
STEP = 10**9
SMALL = pl.CostEstimate(flops=1, bytes_accessed=1, transcendentals=0)
F32 = jnp.float32
BF16 = jnp.bfloat16


def mm(a, b, dims=NN):
    return lax.dot_general(a, b, dims, preferred_element_type=F32)


def attn_kernel(
    half, info_ref, q_ref, doc_ref, own_ref, traded_ref, near_ref, near_traded_ref, far_ref,
    far_traded_ref, fold_near_ref, fold_traded_ref, *refs,
):
    *out_refs, kk, vv, sbuf = refs
    blk = own_ref.shape[1]
    heads = q_ref.shape[2] // HD
    base = info_ref[0]
    hard = info_ref[1] == 1
    easy = info_ref[1] == 0

    def fill(lag, ref):
        rows = pl.ds(lag * blk, blk)
        k = ref[0]
        kk[rows, :] = k
        vv[rows, :HD] = ref[1]
        vv[rows, HD:] = jnp.ones((blk, HD), BF16)

    def choose(lag, cases):
        for condition, ref in cases:
            pl.when(condition)(functools.partial(fill, lag, ref))

    fill(0, own_ref)
    fill(2, near_ref)
    choose(1, ((hard, near_traded_ref), (easy, traded_ref)))
    if half == 0:
        fill(4, far_ref)
        choose(3, ((hard, far_traded_ref), (easy, near_traded_ref)))
    else:
        folded = info_ref[2] == 1
        plain = info_ref[2] == 0
        choose(4, ((folded, fold_traded_ref), (plain, far_ref)))
        choose(3, (
            (jnp.logical_and(hard, plain), far_traded_ref),
            (jnp.logical_and(hard, folded), fold_near_ref),
            (easy, near_traded_ref),
        ))

    factor = HD ** -0.5 * math.log2(math.e)
    tiles = blk // TILE
    far = LAGS * blk
    col = lax.broadcasted_iota(jnp.int32, (TILE, blk), 1)
    row_t = lax.broadcasted_iota(jnp.int32, (TILE, TILE), 0)
    col_t = lax.broadcasted_iota(jnp.int32, (TILE, TILE), 1)
    tri = col_t <= row_t

    def unit(t, a, sb):
        r0 = t * TILE
        cols = slice(a * HD, (a + 1) * HD)
        rel = doc_ref[r0:r0 + TILE, :] - base
        q = q_ref[half, r0:r0 + TILE, cols]
        state = {"m": None, "acc": jnp.zeros((TILE, 2 * HD), F32)}

        def scores(first, count):
            return mm(q, kk[first:first + count, :], NT) * factor

        def keep(s, off):
            for x in range(s.shape[1] // HD):
                p = s[:, x * HD:(x + 1) * HD]
                state["m"] = p if state["m"] is None else jnp.maximum(state["m"], p)
            sb[:, off:off + s.shape[1]] = s

        def whole(lag, off):
            keep(jnp.where(col - lag * blk >= rel, scores(lag * blk, blk), NEG), off)

        def part(lag, u, off):
            s = scores(lag * blk + u * TILE, TILE)
            keep(jnp.where(col_t + (u * TILE - lag * blk) >= rel, s, NEG), off)

        def corner(off):
            s = jnp.where(tri, scores(r0, TILE), scores(far + r0, TILE))
            position = jnp.where(tri, col_t + r0, col_t + (r0 - far))
            keep(jnp.where(position >= rel, s, NEG), off)

        def mix(begin, count, first):
            p = jnp.exp2(sb[:, begin:begin + count] - state["top"]).astype(BF16)
            state["acc"] = state["acc"] + mm(p, vv[first:first + count, :])

        def mix_corner(off):
            p = jnp.exp2(sb[:, off:off + TILE] - state["top"]).astype(BF16)
            zero = jnp.zeros_like(p)
            acc = state["acc"] + mm(jnp.where(tri, p, zero), vv[r0:r0 + TILE, :])
            state["acc"] = acc + mm(jnp.where(tri, zero, p), vv[far + r0:far + r0 + TILE, :])

        def highest():
            state["top"] = jnp.max(state["m"], axis=1, keepdims=True)

        def store():
            acc = state["acc"]
            result = (acc[:, :HD] / acc[:, HD:]).astype(BF16)
            count = out_refs[0].shape[0]
            out_refs[r0 // count][r0 % count:r0 % count + TILE, cols] = result

        first_pass, second_pass = [], []
        off = 0
        for lag in (3, 2, 1):
            first_pass.append(functools.partial(whole, lag, off))
            second_pass.append(functools.partial(mix, off, blk, lag * blk))
            off += blk
        for u in range(tiles):
            if u != t:
                lag = 0 if u < t else LAGS
                first_pass.append(functools.partial(part, lag, u, off))
                second_pass.append(functools.partial(mix, off, TILE, lag * blk + u * TILE))
                off += TILE
        first_pass.append(functools.partial(corner, off))
        second_pass.append(functools.partial(mix_corner, off))
        return first_pass, highest, second_pass, store

    units = [
        unit(t, a, sbuf.at[(t * heads + a) % 2]) for t in range(tiles) for a in range(heads)
    ]
    for step in units[0][0]:
        step()
    units[0][1]()
    for i, (_, _, second_pass, store) in enumerate(units):
        following = units[i + 1][0] if i + 1 < len(units) else []
        for j in range(max(len(following), len(second_pass))):
            if j < len(following):
                following[j]()
            if j < len(second_pass):
                second_pass[j]()
        store()
        if following:
            units[i + 1][1]()


def attention(half, outs, info, q, doc, *blocks):
    _, rows, cols = q.shape
    keys = (LAGS + 1) * rows
    return pl.pallas_call(
        functools.partial(attn_kernel, half),
        out_shape=[jax.ShapeDtypeStruct((rows // outs, cols), BF16)] * outs,
        in_specs=[SMEM] + [VMEM] * (2 + len(blocks)),
        out_specs=[VMEM] * outs,
        scratch_shapes=[
            pltpu.VMEM((keys, HD), BF16),
            pltpu.VMEM((keys, 2 * HD), BF16),
            pltpu.VMEM((2, TILE, LAGS * rows), F32),
        ],
        compiler_params=pltpu.CompilerParams(vmem_limit_bytes=16 * 2**20),
        cost_estimate=pl.CostEstimate(flops=2 * 10**9, bytes_accessed=1, transcendentals=0) if half == 0 else pl.CostEstimate(
            flops=16 * rows * cols * keys, bytes_accessed=4 * 2**20,
            transcendentals=rows * cols // HD * keys,
        ),
        name="attend" + str(half),
    )(info, q, doc, *blocks)


def weights_kernel(info_ref, w_ref, side_ref, far_ref, peer_ref):
    x, y, core = info_ref[0], info_ref[1], info_ref[2]
    rows, wide = far_ref.shape
    width = wide // 2
    ring = peer_ref.shape[0] // rows
    mine = pl.ds(pl.multiple_of(core * rows, rows), rows)

    def columns(first, count):
        return pl.ds(pl.multiple_of(first * count, count), count)

    side_ref[...] = w_ref[:, columns(lax.rem(x + 1 + (ring - 2) * core, ring), wide)]
    far_ref[...] = w_ref[mine, columns(lax.rem(x + 2, ring), wide)]
    for i in range(ring):
        peer_ref[i * rows:(i + 1) * rows, :] = w_ref[mine, columns(2 * i + 1 - y, width)]


def split_weights(info, w, ring):
    rows, cols = w.shape
    return pl.pallas_call(
        weights_kernel,
        out_shape=[
            jax.ShapeDtypeStruct((rows, cols // ring), BF16),
            jax.ShapeDtypeStruct((rows // 2, cols // ring), BF16),
            jax.ShapeDtypeStruct((rows // 2 * ring, cols // ring // 2), BF16),
        ],
        in_specs=[SMEM, VMEM],
        out_specs=[VMEM] * 3,
        compiler_params=pltpu.CompilerParams(vmem_limit_bytes=16 * 2**20),
        cost_estimate=SMALL,
        name="split_weights",
    )(info, w)


def halves(core, rows):
    h = rows // 2
    return pl.ds(pl.multiple_of(core * h, h), h), pl.ds(pl.multiple_of((1 - core) * h, h), h)


def gather_first_kernel(
    info_ref, own_ref, left_ref, right_ref, far_ref, w_ref,
    ws_ref, wsp_ref, wf_ref, wfp_ref, send_ref, keep_ref,
):
    x, y, core = info_ref[0], info_ref[1], info_ref[2]
    rows, width = own_ref.shape
    mine, other = halves(core, width)
    cut = rows // 2

    def block(side, r):
        wide = pl.ds(pl.multiple_of(side * width, width), width)
        own_cols = pl.ds(pl.multiple_of((2 * x + side) * width, width), width)
        left, right = left_ref[r, :], right_ref[r, :]
        acc = mm(own_ref[r, :], w_ref[:, own_cols])
        acc = acc + mm(jnp.where(core == 0, left, right), ws_ref[:, wide])
        acc = acc + mm(jnp.where(core == 0, right, left), wsp_ref[:, wide])
        acc = acc + mm(far_ref[r, mine], wf_ref[:, wide])
        acc = acc + mm(far_ref[r, other], wfp_ref[:, wide])
        return acc.astype(BF16)

    for r in (slice(0, cut), slice(cut, rows)):
        send_ref[r, :] = block(1 - y, r)
    for r in (slice(0, cut), slice(cut, rows)):
        keep_ref[r, :] = block(y, r)


def targets(x, ring):
    return lax.rem(x + 2, ring), lax.rem(x + 1, ring), lax.rem(x + ring - 1, ring), x


def own_part_kernel(info_ref, own_ref, w_ref, part_ref):
    x, y = info_ref[0], info_ref[1]
    width = own_ref.shape[1]
    for i, target in enumerate(targets(x, part_ref.shape[0])):
        cols = pl.ds(pl.multiple_of((2 * target + y) * width, width), width)
        part_ref[i] = mm(own_ref[...], w_ref[:, cols])


def reduce_first_kernel(
    info_ref, peer_ref, part_ref, wm_ref, wp_ref, far_ref, up_ref, down_ref, keep_ref
):
    x, core = info_ref[0], info_ref[2]
    rows, width = peer_ref.shape
    mine, other = halves(core, width)
    h = width // 2
    ring = part_ref.shape[0]
    for i, (ref, target) in enumerate(
        zip((far_ref, up_ref, down_ref, keep_ref), targets(x, ring))
    ):
        w_rows = pl.ds(pl.multiple_of(target * h, h), h)
        for r in (slice(0, rows // 2), slice(rows // 2, rows)):
            acc = part_ref[i, r, :] + mm(peer_ref[r, mine], wm_ref[w_rows, :])
            ref[r, :] = (acc + mm(peer_ref[r, other], wp_ref[w_rows, :])).astype(BF16)


def total_kernel(info_ref, first_ref, *refs):
    *more, o_ref = refs
    total = first_ref[...].astype(F32)
    for ref in more:
        total = total + ref[...].astype(F32)
    o_ref[...] = total.astype(BF16)


def finish_kernel(info_ref, keep_ref, got_ref, done_ref, o_ref):
    o_ref[0] = (keep_ref[...].astype(F32) + got_ref[...].astype(F32)).astype(BF16)
    o_ref[1] = done_ref[...]


def project(kernel, name, outs, args, cost=0):
    return pl.pallas_call(
        kernel,
        out_shape=outs,
        in_specs=[SMEM] + [VMEM] * (len(args) - 1),
        out_specs=[VMEM] * len(outs),
        compiler_params=pltpu.CompilerParams(vmem_limit_bytes=16 * 2**20),
        cost_estimate=pl.CostEstimate(flops=cost, bytes_accessed=1, transcendentals=0),
        name=name,
    )(*args)


def after(array, *others):
    return lax.optimization_barrier((array, *others))[0]


def on_device(query_heads, key_heads, value_heads, doc_start, out_weight):
    ctx_size = lax.axis_size("ctx")
    c = lax.axis_index("ctx")
    head = lax.axis_index("head")
    core = c % 2
    x, y = head // 2, head % 2
    ring = lax.axis_size("head") // 2
    blk = key_heads.shape[1]
    width = query_heads.shape[2]

    def ctx_move(array, to):
        return lax.ppermute(
            array, "ctx", [(i, to(i)) for i in range(ctx_size) if 0 <= to(i) < ctx_size]
        )

    def head_move(array, to):
        return lax.ppermute(array, "head", [(i, to(i)) for i in range(2 * ring)])

    def swap(array):
        return ctx_move(array, lambda i: i ^ 1)

    def plus(array):
        return head_move(array, lambda i: (i + 2) % (2 * ring))

    def minus(array):
        return head_move(array, lambda i: (i - 2) % (2 * ring))

    def across(array):
        return head_move(array, lambda i: (i + 4) % (2 * ring))

    def mirror(array):
        return head_move(array, lambda i: i ^ 1)

    kv0 = jnp.stack([key_heads[0], value_heads[0]])
    kv1 = jnp.stack([key_heads[1], value_heads[1]])
    near0 = ctx_move(kv0, lambda i: i + 2)
    near1 = ctx_move(kv1, lambda i: i - 2)
    traded0 = swap(kv0)
    traded1 = swap(kv1)

    place = jnp.stack([x, y, core]).astype(jnp.int32)
    w_side, w_far, w_peer = split_weights(place, out_weight, ring)
    heads = 2 * ring
    w_side, w_far = after(w_side, traded0, traded1), after(w_far, traded0, traded1)
    w_side = lax.ppermute(w_side, ("ctx", "head"), [
        (i * heads + j, i * heads + (j + (2 if i % 2 == 0 else heads - 2)) % heads)
        for i in range(ctx_size) for j in range(heads)
    ])
    w_far = across(w_far)

    last = c >= ctx_size - 2
    near0 = after(near0, near1, traded0, traded1, w_peer)
    far0 = ctx_move(near0, lambda i: i + 2)
    near0_traded = swap(near0)
    near1 = jnp.where(last, traded0, after(near1, near0))
    far1 = ctx_move(near1, lambda i: i - 2)
    near1_traded = swap(near1)
    far0_traded = swap(far0)
    far1_traded = swap(far1)

    def facts(half):
        block = c if half == 0 else 2 * ctx_size - 1 - c
        info = jnp.stack([block * blk, core == half, last]).astype(jnp.int32)
        return info, query_heads, doc_start[half][:, None]

    w_peer = mirror(after(w_peer, far0))
    [mixed0] = attention(
        0, 1, *facts(0), kv0, traded0, near0, after(near0_traded, near1_traded), far0, far0_traded,
        near0, near0_traded,
    )
    kv1 = after(kv1, mixed0)
    mixed0 = after(mixed0, far1_traded, w_side, w_far)
    left, right, opposite = plus(mixed0), minus(mixed0), across(mixed0)
    [mixed1] = attention(
        1, 1, *facts(1), kv1, traded1, near1, near1_traded, far1, far1_traded, near0, near0_traded
    )
    peer = mirror(mixed1)
    piece = jax.ShapeDtypeStruct((blk, width), BF16)
    [part] = project(
        own_part_kernel, "own_part", [jax.ShapeDtypeStruct((ring, blk, width), F32)],
        [place, after(mixed1, left, right, opposite), out_weight], 8 * STEP,
    )
    w_peer2 = swap(after(w_peer, mixed1))
    far, up, down, keep1 = project(
        reduce_first_kernel, "reduce_first", [piece] * 4, [place, peer, part, w_peer, w_peer2]
    )
    got_far, got_up, got_down = across(far), plus(up), minus(down)
    w_side2, w_far2 = swap(after(w_side, far)), swap(after(w_far, far))
    send, keep0 = project(
        gather_first_kernel, "gather_first", [piece] * 2,
        [place, mixed0, left, right, opposite, out_weight, w_side, w_side2, w_far, w_far2],
    )
    got0 = mirror(send)
    [out1] = project(
        total_kernel, "total", [piece], [place, keep1, got_far, got_up, got_down], STEP
    )
    return project(
        finish_kernel, "finish", [jax.ShapeDtypeStruct((2, blk, width), BF16)],
        [place, keep0, got0, out1],
    )[0]


def solution(mesh):
    in_specs = (
        P(None, "ctx", "head"),
        P(None, "ctx", "head"),
        P(None, "ctx", "head"),
        P(None, "ctx"),
        P("head", None),
    )
    out_specs = P(None, "ctx", "head")
    return jax.shard_map(
        on_device, mesh=mesh, in_specs=in_specs, out_specs=out_specs, check_vma=False
    )
```
